32 devices in a mesh: feat: 16 (over z, y, x), samp: 2 (over core).
Axes of the slice: x: 2, y: 2, z: 4, core: 2. Of those that a mesh axis runs over, the one named last changes fastest.
Arguments:
- spectra: bfloat16 [16384, 512], P('feat', 'samp'), may hold values from -6 to 6
- pair_blocks: int32 [512, 2], P('feat'), may hold values from -1 to 63, as said below
- windows: int32 [64, 2], replicated, may hold values from 0 to 2998, as said below
Outputs:
- corr: float32 [512, 256, 256], P(('feat', 'samp'))
- profiles: bfloat16 [16384, 512], P('feat', 'samp')
The draws below stay inside these ranges and needn't reach their ends.
Inputs may be any that keep to these rules, and one draw needn't show every extreme that they name: `pair_blocks`: slots lie in groups of 8; slot s of the device at index d along feat is in group g = s // 8. A live entry (i, j) has block i among the 4 blocks of device d and block j among those of device d + g, with i <= j in group 0; no pair appears twice; unused slots hold -1 in both columns. At most 8 slots of a group are live, and some group has all 8 live. `windows`: column 0 is a block's first retention index and column 1 its last, which is at least 20 larger.
All inputs are finite; a program needn't handle non-finite values.
Results may differ from the reference program's by a relative error of at most 0.0075.
Values may be sent and summed in bfloat16 or wider, within the bound.
No kernel may reach another device: no remote copies, remote signals or barrier semaphores. Data moves between devices by JAX's collectives and lax.ppermute only.
A program may use at most 64 MiB of HBM per device.

```python
import jax
import jax.numpy as jnp
import numpy as np
from jax import lax

BS = 256
BLK_DEV = 4
CAP = 8
REACH = 3
SLOTS = 32
SAMPLES = 512
NBLK = 64
FEATS = 16384
NPAIR = 512


def draw_pair_blocks(key, part):
    nfeat = NBLK // BLK_DEV
    upper = [(a, b) for a in range(BLK_DEV) for b in range(BLK_DEV) if a <= b]
    every = [(a, b) for a in range(BLK_DEV) for b in range(BLK_DEV)]
    upper_a = jnp.array(np.array([p[0] for p in upper], dtype=np.int32))
    upper_b = jnp.array(np.array([p[1] for p in upper], dtype=np.int32))
    every_a = jnp.array(np.array([p[0] for p in every], dtype=np.int32))
    every_b = jnp.array(np.array([p[1] for p in every], dtype=np.int32))
    count_upper = len(upper)
    count_every = len(every)

    def one_group(index):
        device = index // (REACH + 1)
        group = index % (REACH + 1)
        local = jax.random.fold_in(key, index)
        order_upper = jax.random.permutation(jax.random.fold_in(local, 1), count_upper)[:CAP]
        order_every = jax.random.permutation(jax.random.fold_in(local, 2), count_every)[:CAP]
        first_local = jnp.where(group == 0, upper_a[order_upper], every_a[order_every])
        second_local = jnp.where(group == 0, upper_b[order_upper], every_b[order_every])
        livecount = jax.random.randint(jax.random.fold_in(local, 3), (), 2, CAP + 1)
        livecount = jnp.where((device == 0) & (group == 1), CAP, livecount)
        livecount = jnp.where(device + group >= nfeat, 0, livecount)
        alive = jnp.arange(CAP) < livecount
        first = jnp.where(alive, device * BLK_DEV + first_local, -1)
        second = jnp.where(alive, (device + group) * BLK_DEV + second_local, -1)
        return jnp.stack([first, second], axis=1)
    table = jax.vmap(one_group)(jnp.arange(nfeat * (REACH + 1)))
    return table.reshape(nfeat * (REACH + 1) * CAP, 2).astype(jnp.int32)


def draw_windows(key, part):
    blocks = jnp.arange(NBLK, dtype=jnp.int32)
    start = 40 * blocks + jax.random.randint(jax.random.fold_in(key, 11), (NBLK,), 0, 40)
    extent = jax.random.randint(jax.random.fold_in(key, 12), (NBLK,), 20, 400)
    return jnp.stack([start, start + extent], axis=1).astype(jnp.int32)


def levels(key, dims, shards, smallest, top_value):
    gain, own = 1.0, jax.random.fold_in(key, 6)
    for position, blocks in shards:
        draws = jnp.exp(jax.random.uniform(jax.random.fold_in(own, position), (blocks,), jnp.float32, smallest / len(shards), top_value / len(shards)))
        gain = gain * jnp.repeat(draws, dims[position] // blocks).reshape([-1 if axis == position else 1 for axis in range(len(dims))])
    return gain


def gaussian(stream_key, shape, deviation, most, pieces=(), kind=jnp.bfloat16):
    values = deviation * jax.random.normal(stream_key, shape, jnp.float32)
    if pieces:
        values = values * levels(stream_key, shape, pieces, -0.22, 0.18)
    return jnp.clip(values, -most, most).astype(kind)


def setup_inputs(seed: int = 0) -> dict:
    keys = jax.random.split(jax.random.key(seed), 4)
    spectra = gaussian(keys[0], (FEATS, SAMPLES), 1.0, 6.0, ((0, 16), (1, 2)))
    pair_blocks = draw_pair_blocks(jax.random.fold_in(keys[3], 71), 0)
    windows = draw_windows(jax.random.fold_in(keys[3], 71), 0)
    return {"spectra": spectra, "pair_blocks": pair_blocks, "windows": windows}


def reference(spectra, pair_blocks, windows):
    values = spectra.astype(jnp.float32)
    mean = lax.optimization_barrier(jnp.sum(values, axis=1)) / SAMPLES
    var = lax.optimization_barrier(jnp.sum(values * values, axis=1)) / SAMPLES - mean * mean
    inv = lax.rsqrt(var + 1e-05)
    z = ((values - mean[:, None]) * inv[:, None]).astype(jnp.bfloat16)
    zb = z.reshape(NBLK, BS, SAMPLES)
    first = pair_blocks[:, 0]
    second = pair_blocks[:, 1]
    live = first >= 0
    ia = jnp.maximum(first, 0)
    ja = jnp.maximum(second, 0)
    lo_i = windows[ia, 0]
    hi_i = windows[ia, 1]
    lo_j = windows[ja, 0]
    hi_j = windows[ja, 1]
    intersection = jnp.maximum(jnp.minimum(hi_i, hi_j) - jnp.maximum(lo_i, lo_j), 0)
    weight = (intersection + 16).astype(jnp.float32) / (hi_i - lo_i + hi_j - lo_j + 16).astype(jnp.float32)
    weight = jnp.where(live, weight, jnp.float32(0.0))

    def tile_of(args):
        ci, cj, cw = args
        gram = jnp.einsum('pfs,pgs->pfg', zb[ci].astype(jnp.float32), zb[cj].astype(jnp.float32))
        return gram * (cw / SAMPLES)[:, None, None]
    corr = lax.map(tile_of, (ia.reshape(-1, SLOTS), ja.reshape(-1, SLOTS), weight.reshape(-1, SLOTS)))
    tiles = corr.astype(jnp.bfloat16)
    corr = corr.reshape(NPAIR, BS, BS)

    def accumulate(acc, args):
        ci, cj, ct = args
        ct32 = ct.astype(jnp.float32)
        ahead = jnp.einsum('pfg,pgs->pfs', ct32, zb[cj].astype(jnp.float32))
        acc = acc.at[ci].add(ahead)
        differ = (ci != cj).astype(jnp.float32)
        behind = jnp.einsum('pfg,pfs->pgs', ct32, zb[ci].astype(jnp.float32)) * differ[:, None, None]
        acc = acc.at[cj].add(behind)
        return (acc, None)
    acc, _ = lax.scan(accumulate, zb.astype(jnp.float32), (ia.reshape(-1, SLOTS), ja.reshape(-1, SLOTS), tiles))
    profiles = acc.astype(jnp.bfloat16).reshape(FEATS, SAMPLES)
    return (corr, profiles)
```

```python
import functools

import jax
import jax.numpy as jnp
from jax import lax
from jax.experimental import pallas as pl
from jax.experimental.pallas import tpu as pltpu
from jax.sharding import PartitionSpec as P

BS = 256
BLK_DEV = 4
CAP = 8
REACH = 3
QUAD = 4
EPS = 1e-05
VMEM = 24 * 1024 * 1024


def along_x(i):
    return i ^ 1


def along_y(i):
    return i ^ 2


def along_z_own(i):
    return i - QUAD if i % 2 == 0 else i + QUAD


def along_z_side(i):
    return i + QUAD if i % QUAD < 2 else i - QUAD


def send(value, move):
    length = lax.axis_size("feat")
    pairs = [(i, move(i)) for i in range(length) if 0 <= move(i) < length]
    return lax.ppermute(value, "feat", pairs)


def swap(value):
    return lax.ppermute(value, "samp", [(0, 1), (1, 0)])


def off_x(r):
    return 1 - 2 * (r % 2)


def off_y(r):
    return 2 - 4 * (r // 2)


def off_diag(r):
    return 3 - 2 * r


def off_zx(r):
    return 6 * (r % 2) - 3


def off_zy(r):
    return 4 * (r // 2) - 2


def off_last(r):
    return jnp.where(r == 0, -1, jnp.where(r == 1, -3, jnp.where(r == 2, 3, 1)))


def normalise(own_ref, par_ref, z_ref, start):
    rows, width = own_ref.shape
    step = 128

    def one(k, _):
        at = pl.multiple_of(k * step, step)
        a = own_ref[pl.ds(at, step), :].astype(jnp.float32)
        b = par_ref[pl.ds(at, step), :].astype(jnp.float32)
        total = 2 * width
        mean = jnp.sum(a + b, axis=1, keepdims=True) / total
        var = jnp.sum(a * a + b * b, axis=1, keepdims=True) / total - mean * mean
        inv = lax.rsqrt(var + EPS)
        to = pl.multiple_of(start + k * step, step)
        z_ref[pl.ds(to, step), :width] = ((a - mean) * inv).astype(jnp.bfloat16)
        z_ref[pl.ds(to, step), width:] = ((b - mean) * inv).astype(jnp.bfloat16)
        return 0

    lax.fori_loop(0, rows // step, one, 0)


def slot_of(meta, wins, off, slot):
    position = meta[0]
    at = 2 + ((off + REACH) * CAP + slot) * 2
    mine = meta[at]
    other = meta[at + 1]
    live = mine >= 0
    b = jnp.where(live, mine - position * BLK_DEV, 0)
    o = jnp.where(live, other - (position + off) * BLK_DEV, 0)
    mine = jnp.maximum(mine, 0)
    other = jnp.maximum(other, 0)
    lo_b = wins[2 * mine]
    hi_b = wins[2 * mine + 1]
    lo_o = wins[2 * other]
    hi_o = wins[2 * other + 1]
    meet = jnp.maximum(jnp.minimum(hi_b, hi_o) - jnp.maximum(lo_b, lo_o), 0)
    num = jnp.where(live, meet + 16, 0)
    den = hi_b - lo_b + hi_o - lo_o + 16
    return b, o, num, den


def scale_of(num, den, samples):
    top = jnp.full((1, BS), num, jnp.int32).astype(jnp.float32)
    low = jnp.full((1, BS), den, jnp.int32).astype(jnp.float32)
    return top / low / samples


def block(ref, index):
    return ref[pl.ds(pl.multiple_of(index * BS, BS), BS), :]


def pair_slots(meta, wins, off, zown_ref, z_ref, acc_ref, tile_ref, itself):
    width = acc_ref.shape[1]
    samples = 2 * width

    def one(slot, _):
        b, o, num, den = slot_of(meta, wins, off, slot)
        scale = scale_of(num, den, samples)
        zb = block(zown_ref, b)
        zo = block(z_ref, o)
        gram = lax.dot_general(
            zb, zo, (((1,), (1,)), ((), ())), preferred_element_type=jnp.float32
        )
        corr = gram * scale
        tile_ref[slot] = corr
        tile = corr.astype(jnp.bfloat16)
        at = pl.ds(pl.multiple_of(b * BS, BS), BS)
        acc_ref[at, :] += jnp.dot(tile, zo[:, :width], preferred_element_type=jnp.float32)
        if itself:
            differ = jnp.where(b == o, 0.0, 1.0)
            back = lax.dot_general(
                tile, zb[:, :width], (((0,), (0,)), ((), ())), preferred_element_type=jnp.float32
            )
            at = pl.ds(pl.multiple_of(o * BS, BS), BS)
            acc_ref[at, :] += back * differ
        return 0

    lax.fori_loop(0, CAP, one, 0)


def put_tiles(meta, off, tile_ref, corr_ref, sem):
    mine = jnp.logical_and(off >= 0, off // 2 == meta[1])
    first = pl.multiple_of(jnp.where(off == 1, CAP, jnp.where(off == 3, CAP, 0)), CAP)
    copy = pltpu.make_async_copy(tile_ref, corr_ref.at[pl.ds(first, CAP)], sem)
    return mine, copy


def self_kernel(meta, wins, own_ref, par_ref, zown_ref, acc_ref, corr_ref, tile_ref, sem):
    width = own_ref.shape[1]
    normalise(own_ref, par_ref, zown_ref, 0)
    acc_ref[...] = zown_ref[:, :width].astype(jnp.float32)
    pair_slots(meta, wins, 0, zown_ref, zown_ref, acc_ref, tile_ref, True)
    mine, copy = put_tiles(meta, jnp.int32(0), tile_ref, corr_ref, sem)

    @pl.when(mine)
    def _():
        copy.start()
        copy.wait()


def unit_kernel(offs, pieces, final, *refs):
    count = len(offs)
    meta, wins, zown_ref, acc_in = refs[:4]
    raws = refs[4 : 4 + 2 * count * pieces]
    rest = refs[4 + 2 * count * pieces + 1 :]
    out_ref, corr_ref, acc_ref, z_ref, tile_ref, sems = rest
    acc_ref[...] = acc_in[...]
    r = lax.rem(meta[0], QUAD)
    pending = []
    for k, off_of in enumerate(offs):
        off = off_of(r)
        start = 0
        for piece in range(pieces):
            own_ref, par_ref = raws[2 * (k * pieces + piece) : 2 * (k * pieces + piece) + 2]
            normalise(own_ref, par_ref, z_ref, start)
            start += own_ref.shape[0]
        if k >= 2:
            was, before = pending[k - 2]

            @pl.when(was)
            def _(before=before):
                before.wait()

        tiles = tile_ref.at[k % 2]
        pair_slots(meta, wins, off, zown_ref, z_ref, acc_ref, tiles, False)
        mine, copy = put_tiles(meta, off, tiles, corr_ref, sems.at[k % 2])
        pending.append((mine, copy))

        @pl.when(mine)
        def _(copy=copy):
            copy.start()

    out_ref[...] = acc_ref[...].astype(out_ref.dtype)
    for was, before in pending[-2:]:

        @pl.when(was)
        def _(before=before):
            before.wait()


def estimate(units):
    return pl.CostEstimate(
        flops=units * CAP * 2 * BS * BS * BS * 3, bytes_accessed=units * 8 * 2**20, transcendentals=0
    )


SMEM = pl.BlockSpec(memory_space=pltpu.SMEM)
INSIDE = pl.BlockSpec(memory_space=pltpu.VMEM)
ANY = pl.BlockSpec(memory_space=pl.ANY)


def run_self(meta, wins, own, par):
    rows, width = own.shape
    return pl.pallas_call(
        self_kernel,
        out_shape=(
            jax.ShapeDtypeStruct((rows, 2 * width), jnp.bfloat16),
            jax.ShapeDtypeStruct((rows, width), jnp.float32),
            jax.ShapeDtypeStruct((2 * CAP, BS, BS), jnp.float32),
        ),
        in_specs=[SMEM, SMEM, INSIDE, INSIDE],
        out_specs=(INSIDE, INSIDE, ANY),
        scratch_shapes=[pltpu.VMEM((CAP, BS, BS), jnp.float32), pltpu.SemaphoreType.DMA],
        compiler_params=pltpu.CompilerParams(vmem_limit_bytes=VMEM),
        cost_estimate=estimate(1),
        name="self_pairs",
    )(meta, wins, own, par)


def run_units(meta, wins, zown, acc, corr, offs, raws, pieces, final):
    rows, width = acc.shape
    name = "last_pairs" if final else "unit_pairs"
    return pl.pallas_call(
        functools.partial(unit_kernel, offs, pieces, final),
        out_shape=(
            jax.ShapeDtypeStruct((rows, width), jnp.bfloat16 if final else jnp.float32),
            jax.ShapeDtypeStruct(corr.shape, corr.dtype),
        ),
        in_specs=[SMEM, SMEM, INSIDE, INSIDE] + [INSIDE] * len(raws) + [ANY],
        out_specs=(INSIDE, ANY),
        scratch_shapes=[
            pltpu.VMEM((rows, width), jnp.float32),
            pltpu.VMEM((rows, 2 * width), jnp.bfloat16),
            pltpu.VMEM((2, CAP, BS, BS), jnp.float32),
            pltpu.SemaphoreType.DMA((2,)),
        ],
        input_output_aliases={4 + len(raws): 1},
        compiler_params=pltpu.CompilerParams(vmem_limit_bytes=VMEM),
        cost_estimate=estimate(len(offs)),
        name=name,
    )(meta, wins, zown, acc, *raws, corr)


def body(spectra, pair_blocks, windows):
    position = lax.axis_index("feat")
    half = spectra.shape[0] // 2
    par = swap(spectra)
    from_x = send(spectra, along_x)
    from_y = send(spectra, along_y)
    from_z = send(spectra, along_z_own)
    groups = pair_blocks.reshape(REACH + 1, CAP, 2)
    behind = [send(groups[g], lambda i, g=g: i + g) for g in range(1, REACH + 1)]
    tables = [
        jnp.where(position >= g, behind[g - 1][:, ::-1], -1) for g in range(REACH, 0, -1)
    ]
    ids = jnp.stack([position, lax.axis_index("samp")]).astype(jnp.int32)
    none = jnp.full((REACH * CAP * 2,), -1, jnp.int32)
    wins = windows.reshape(-1)
    meta0 = jnp.concatenate([ids, none, pair_blocks.reshape(-1)])
    zown, acc, corr = run_self(meta0, wins, spectra, par)
    meta = jnp.concatenate([ids] + [t.reshape(-1) for t in tables] + [pair_blocks.reshape(-1)])
    diag = send(from_x, along_y)
    zx = send(from_z, along_x)
    zy = send(from_y, along_z_side)
    raws = (from_x, swap(from_x), from_y, swap(from_y))
    acc, corr = run_units(meta, wins, zown, acc, corr, (off_x, off_y), raws, 1, False)
    last_a = send(zy[:half], along_x)
    last_b = send(diag[half:], along_z_side)
    raws = (diag, swap(diag), zx, swap(zx), zy, swap(zy))
    acc, corr = run_units(meta, wins, zown, acc, corr, (off_diag, off_zx, off_zy), raws, 1, False)
    raws = (last_a, swap(last_a), last_b, swap(last_b))
    profiles, corr = run_units(meta, wins, zown, acc, corr, (off_last,), raws, 2, True)
    return (corr, profiles)


def solution(mesh):
    placed = (P("feat", "samp"), P("feat", None), P())
    return jax.shard_map(
        body,
        mesh=mesh,
        in_specs=placed,
        out_specs=(P(("feat", "samp"), None, None), P("feat", "samp")),
        check_vma=False,
    )
```

```python
import functools

import jax
import jax.numpy as jnp
from jax import lax
from jax.experimental import pallas as pl
from jax.experimental.pallas import tpu as pltpu
from jax.sharding import PartitionSpec as P

BS = 256
BLK_DEV = 4
CAP = 8
REACH = 3
QUAD = 4
EPS = 1e-05
STEP = 256
TABLE = 2 * CAP
VMEM = 24 * 1024 * 1024


def along_x(i, n):
    return i ^ 1


def along_y(i, n):
    return i ^ 2


def along_z_own(i, n):
    return (i - QUAD if i % 2 == 0 else i + QUAD) % n


def along_z_side(i, n):
    return (i + QUAD if i % QUAD < 2 else i - QUAD) % n


def send(value, move):
    length = lax.axis_size("feat")
    return lax.ppermute(value, "feat", [(i, move(i, length)) for i in range(length)])


def swap(value):
    return lax.ppermute(value, "samp", [(0, 1), (1, 0)])


def off_self(r):
    return 0 * r


def off_x(r):
    return 1 - 2 * lax.rem(r, 2)


def off_y(r):
    return 2 - 4 * lax.div(r, 2)


def off_diag(r):
    return 3 - 2 * r


def off_zx(r):
    return 6 * lax.rem(r, 2) - 3


def off_zy(r):
    return 4 * lax.div(r, 2) - 2


def off_last(r):
    return jnp.where(r == 0, -1, jnp.where(r == 1, -3, jnp.where(r == 2, 3, 1)))


def normalise(own_ref, par_ref, z_ref, start, rows):
    width = own_ref.shape[1]
    total = 2 * width
    for at in range(0, rows, STEP):
        a = own_ref[at : at + STEP, :].astype(jnp.float32)
        b = par_ref[at : at + STEP, :].astype(jnp.float32)
        mean = jnp.sum(a + b, axis=1, keepdims=True) / total
        var = jnp.sum(a * a + b * b, axis=1, keepdims=True) / total - mean * mean
        inv = lax.rsqrt(var + EPS)
        to = slice(start + at, start + at + STEP)
        z_ref[to, :width] = ((a - mean) * inv).astype(jnp.bfloat16)
        z_ref[to, width:] = ((b - mean) * inv).astype(jnp.bfloat16)


def slot_of(meta, wins, off, slot, code):
    position = meta[0]
    ahead = off >= 0
    at = 2 + (jnp.maximum(off, 0) * CAP + slot) * 2
    left = jnp.where(ahead, meta[at] - position * BLK_DEV, lax.div(code, BLK_DEV))
    right = jnp.where(ahead, meta[at + 1] - (position + off) * BLK_DEV, lax.rem(code, BLK_DEV))
    live = jnp.where(ahead, meta[at], code) >= 0
    live = jnp.logical_and(live, position + off >= 0)
    b = jnp.where(live, jnp.where(ahead, left, right), 0)
    o = jnp.where(live, jnp.where(ahead, right, left), 0)
    mine = position * BLK_DEV + b
    other = jnp.where(live, (position + off) * BLK_DEV + o, 0)
    lo_b = wins[2 * mine]
    hi_b = wins[2 * mine + 1]
    lo_o = wins[2 * other]
    hi_o = wins[2 * other + 1]
    meet = jnp.maximum(jnp.minimum(hi_b, hi_o) - jnp.maximum(lo_b, lo_o), 0)
    num = jnp.where(live, meet + 16, 0)
    den = hi_b - lo_b + hi_o - lo_o + 16
    return b, o, num, den


def codes_of(table, off):
    values = table.astype(jnp.float32)
    row = lax.broadcasted_iota(jnp.int32, values.shape, 0)
    lane = lax.broadcasted_iota(jnp.int32, values.shape, 1)
    first = jnp.where(off == -2, CAP, 0)
    column = jnp.where(off == -3, 1, 0)
    return [
        jnp.sum(
            jnp.where(jnp.logical_and(row == first + slot, lane == column), values, 0.0)
        ).astype(jnp.int32)
        for slot in range(CAP)
    ]


def scale_of(num, den, samples):
    top = jnp.full((1, BS), num, jnp.int32).astype(jnp.float32)
    low = jnp.full((1, BS), den, jnp.int32).astype(jnp.float32)
    return top / low / samples


def at_block(index):
    return pl.ds(pl.multiple_of(index * BS, BS), BS)


def grams(meta, wins, off, codes, zown_ref, z_ref, tile_ref):
    samples = zown_ref.shape[1]
    found = [slot_of(meta, wins, off, slot, codes[slot]) for slot in range(CAP)]
    for slot, (b, o, num, den) in enumerate(found):
        gram = lax.dot_general(
            zown_ref[at_block(b), :],
            z_ref[at_block(o), :],
            (((1,), (1,)), ((), ())),
            preferred_element_type=jnp.float32,
        )
        tile_ref[slot] = gram * scale_of(num, den, samples)
    return found


def products(found, zown_ref, z_ref, tile_ref, acc_ref, itself):
    width = acc_ref.shape[1]
    for slot, (b, o, _, _) in enumerate(found):
        tile = tile_ref[slot].astype(jnp.bfloat16)
        acc_ref[at_block(b), :] += jnp.dot(
            tile, z_ref[at_block(o), :width], preferred_element_type=jnp.float32
        )
        if itself:
            back = lax.dot_general(
                tile,
                zown_ref[at_block(b), :width],
                (((0,), (0,)), ((), ())),
                preferred_element_type=jnp.float32,
            )
            acc_ref[at_block(o), :] += back * jnp.where(b == o, 0.0, 1.0)


def put_tiles(meta, off, tile_ref, corr_ref, sem):
    mine = jnp.logical_and(off >= 0, lax.div(off, 2) == meta[1])
    first = jnp.where(jnp.logical_or(off == 1, off == 3), CAP, 0)
    copy = pltpu.make_async_copy(
        tile_ref, corr_ref.at[pl.ds(pl.multiple_of(first, CAP), CAP)], sem
    )

    @pl.when(mine)
    def _():
        copy.start()

    return mine, copy


def end_tiles(pending):
    mine, copy = pending

    @pl.when(mine)
    def _():
        copy.wait()


def self_kernel(meta, wins, own_ref, par_ref, zown_ref, acc_ref, corr_ref, tile_ref, sem):
    width = own_ref.shape[1]
    normalise(own_ref, par_ref, zown_ref, 0, own_ref.shape[0])
    found = grams(meta, wins, jnp.int32(0), [jnp.int32(-1)] * CAP, zown_ref, zown_ref, tile_ref)
    pending = put_tiles(meta, jnp.int32(0), tile_ref, corr_ref, sem)
    acc_ref[...] = zown_ref[:, :width].astype(jnp.float32)
    products(found, zown_ref, zown_ref, tile_ref, acc_ref, True)
    end_tiles(pending)


def unit_kernel(offs, pieces, *refs):
    count = len(offs)
    meta, wins, zown_ref, acc_in = refs[:4]
    raws = refs[4 : 4 + 2 * count * pieces]
    out_ref, corr_ref, acc_ref, z_ref, tile_ref, sems = refs[4 + 2 * count * pieces + 1 :]
    rows = acc_in.shape[0]
    acc_ref[...] = acc_in[...]
    r = lax.rem(meta[0], QUAD)
    pending = []
    for k, off_of in enumerate(offs):
        off = off_of(r)
        start = 0
        zs, tiles = z_ref.at[k], tile_ref.at[k]
        for piece in range(pieces):
            own_ref, par_ref = raws[2 * (k * pieces + piece) : 2 * (k * pieces + piece) + 2]
            count_rows = min(own_ref.shape[0], rows - start)
            normalise(own_ref, par_ref, zs, start, count_rows)
            start += count_rows
        table = own_ref[count_rows : count_rows + TABLE, :128]
        codes = codes_of(table, off)
        found = grams(meta, wins, off, codes, zown_ref, zs, tiles)
        pending.append(put_tiles(meta, off, tiles, corr_ref, sems.at[k]))
        products(found, zown_ref, zs, tiles, acc_ref, False)
    out_ref[...] = acc_ref[...].astype(out_ref.dtype)
    for one in pending:
        end_tiles(one)


def estimate(units):
    return pl.CostEstimate(
        flops=units * CAP * 2 * BS * BS * BS * 3, bytes_accessed=units * 8 * 2**20, transcendentals=0
    )


SMEM = pl.BlockSpec(memory_space=pltpu.SMEM)
INSIDE = pl.BlockSpec(memory_space=pltpu.VMEM)
ANY = pl.BlockSpec(memory_space=pl.ANY)


def run_self(meta, wins, own, par):
    rows, width = own.shape
    return pl.pallas_call(
        self_kernel,
        out_shape=(
            jax.ShapeDtypeStruct((rows, 2 * width), jnp.bfloat16),
            jax.ShapeDtypeStruct((rows, width), jnp.float32),
            jax.ShapeDtypeStruct((2 * CAP, BS, BS), jnp.float32),
        ),
        in_specs=[SMEM, SMEM, INSIDE, INSIDE],
        out_specs=(INSIDE, INSIDE, ANY),
        scratch_shapes=[pltpu.VMEM((CAP, BS, BS), jnp.float32), pltpu.SemaphoreType.DMA],
        compiler_params=pltpu.CompilerParams(vmem_limit_bytes=VMEM),
        cost_estimate=estimate(1),
        name="self_pairs",
    )(meta, wins, own, par)


def run_units(meta, wins, zown, acc, corr, offs, raws, pieces=1, final=False):
    rows, width = acc.shape
    count = len(offs)
    return pl.pallas_call(
        functools.partial(unit_kernel, offs, pieces),
        out_shape=(
            jax.ShapeDtypeStruct((rows, width), jnp.bfloat16 if final else jnp.float32),
            jax.ShapeDtypeStruct(corr.shape, corr.dtype),
        ),
        in_specs=[SMEM, SMEM, INSIDE, INSIDE] + [INSIDE] * len(raws) + [ANY],
        out_specs=(INSIDE, ANY),
        scratch_shapes=[
            pltpu.VMEM((rows, width), jnp.float32),
            pltpu.VMEM((count, rows, 2 * width), jnp.bfloat16),
            pltpu.VMEM((count, CAP, BS, BS), jnp.float32),
            pltpu.SemaphoreType.DMA((count,)),
        ],
        input_output_aliases={4 + len(raws): 1},
        compiler_params=pltpu.CompilerParams(vmem_limit_bytes=VMEM),
        cost_estimate=estimate(count),
        name="last_pairs" if final else "unit_pairs",
    )(meta, wins, zown, acc, *raws, corr)


def with_table(spectra, pair_blocks, position):
    first = pair_blocks[:, :1] - position * BLK_DEV
    group = lax.broadcasted_iota(jnp.int32, first.shape, 0) // CAP
    second = pair_blocks[:, 1:] - (position + group) * BLK_DEV
    code = jnp.where(pair_blocks[:, :1] >= 0, first * BLK_DEV + second, -1).astype(spectra.dtype)
    width = spectra.shape[1]
    near = jnp.pad(code[CAP : 3 * CAP], ((0, 0), (0, width - 1)))
    far = jnp.pad(code[3 * CAP :], ((0, CAP), (1, width - 2)))
    return jnp.concatenate([spectra, near + far], axis=0)


def body(spectra, pair_blocks, windows):
    hold = lax.optimization_barrier
    position = lax.axis_index("feat")
    half = spectra.shape[0] // 2
    par = swap(spectra)
    unit = with_table(spectra, pair_blocks, position)
    from_y = send(unit, along_y)
    from_x = send(unit, along_x)
    from_z = send(unit, along_z_own)
    ids = jnp.stack([position, lax.axis_index("samp")]).astype(jnp.int32)
    meta = jnp.concatenate([ids, pair_blocks.reshape(-1)])
    wins = windows.reshape(-1)
    zown, acc, corr = run_self(meta, wins, spectra, par)
    from_x, from_y, acc = hold((from_x, from_y, acc))
    diag = send(from_x, along_y)
    zy = send(from_y, along_z_side)
    from_z, acc = hold((from_z, acc))
    zx = send(from_z, along_x)
    raws = (from_x, swap(from_x), from_y, swap(from_y))
    acc, corr = run_units(meta, wins, zown, acc, corr, (off_x, off_y), raws)
    diag, acc = hold((diag, acc))
    last_a = send(diag[:half], along_z_side)
    zy, zx, acc = hold((zy, zx, acc))
    last_b = send(zy[half:], along_x)
    raws = (diag, swap(diag), zy, swap(zy), zx, swap(zx))
    acc, corr = run_units(meta, wins, zown, acc, corr, (off_diag, off_zy, off_zx), raws)
    last_a, last_b, acc = hold((last_a, last_b, acc))
    raws = (last_a, swap(last_a), last_b, swap(last_b))
    profiles, corr = run_units(meta, wins, zown, acc, corr, (off_last,), raws, 2, True)
    return (corr, profiles)


def solution(mesh):
    placed = (P("feat", "samp"), P("feat", None), P())
    return jax.shard_map(
        body,
        mesh=mesh,
        in_specs=placed,
        out_specs=(P(("feat", "samp"), None, None), P("feat", "samp")),
        check_vma=False,
    )
```

```python
import functools

import jax
import jax.numpy as jnp
from jax import lax
from jax.experimental import pallas as pl
from jax.experimental.pallas import tpu as pltpu
from jax.sharding import PartitionSpec as P

BS = 256
BLK_DEV = 4
CAP = 8
REACH = 3
SLOTS = (REACH + 1) * CAP
QUAD = 4
EPS = 1e-05
STEP = 256
TABLE = 2 * CAP
VMEM = 24 * 1024 * 1024


def along_x(i):
    return i ^ 1


def along_y(i):
    return i ^ 2


def along_z_side(i, n):
    return (i + QUAD if i % QUAD < 2 else i - QUAD) % n


def move_near(i, core, n):
    return (along_x(i), 0) if core == 0 else (along_y(i), 1)


def move_z(i, core, n):
    return (i - QUAD if i % 2 == 0 else i + QUAD) % n, core


def move_next(i, core, n):
    if core == 0:
        to = along_y(i)
        return to, (1 if to % QUAD == 0 else 0)
    to = along_z_side(i, n)
    return to, (0 if to % QUAD == 0 else 1)


def move_x(i, core, n):
    return along_x(i), core


def move_last(i, core, n):
    holds_diag = core == (1 if i % QUAD == 0 else 0)
    return (along_z_side(i, n), 0) if holds_diag else (along_x(i), 1)


def send(value, move):
    length, cores = lax.axis_size("feat"), lax.axis_size("samp")
    pairs = []
    for i in range(length):
        for core in range(cores):
            to, to_core = move(i, core, length)
            pairs.append((i * cores + core, to * cores + to_core))
    return lax.ppermute(value, ("feat", "samp"), pairs)


def swap(value):
    return lax.ppermute(value, "samp", [(0, 1), (1, 0)])


def off_near(r, core):
    return jnp.where(core == 0, 1 - 2 * lax.rem(r, 2), 2 - 4 * lax.div(r, 2))


def off_next(r, core):
    return jnp.where((core == 0) != (r == 0), 3 - 2 * r, 4 * lax.div(r, 2) - 2)


def off_zx(r, core):
    return 6 * lax.rem(r, 2) - 3


def off_last(r, core):
    return jnp.where(r == 0, -1, jnp.where(r == 1, -3, jnp.where(r == 2, 3, 1)))


def normalise(read_own, read_par, z_ref):
    rows = z_ref.shape[0]
    width = z_ref.shape[1] // 2
    total = 2 * width
    for at in range(0, rows, STEP):
        here = slice(at, at + STEP)
        a = read_own(here).astype(jnp.float32)
        b = read_par(here).astype(jnp.float32)
        mean = jnp.sum(a + b, axis=1, keepdims=True) / total
        var = jnp.sum(a * a + b * b, axis=1, keepdims=True) / total - mean * mean
        inv = lax.rsqrt(var + EPS)
        z_ref[here, :width] = ((a - mean) * inv).astype(jnp.bfloat16)
        z_ref[here, width:] = ((b - mean) * inv).astype(jnp.bfloat16)


def slot_of(ids, table, wins, off, slot, code):
    position = ids[0]
    ahead = off >= 0
    at = jnp.maximum(off, 0) * CAP + slot
    left = jnp.where(ahead, table[0, at] - position * BLK_DEV, lax.div(code, BLK_DEV))
    right = jnp.where(ahead, table[1, at] - (position + off) * BLK_DEV, lax.rem(code, BLK_DEV))
    live = jnp.where(ahead, table[0, at], code) >= 0
    live = jnp.logical_and(live, position + off >= 0)
    b = jnp.where(live, jnp.where(ahead, left, right), 0)
    o = jnp.where(live, jnp.where(ahead, right, left), 0)
    mine = position * BLK_DEV + b
    other = jnp.where(live, (position + off) * BLK_DEV + o, 0)
    lo_b, hi_b = wins[0, mine], wins[1, mine]
    lo_o, hi_o = wins[0, other], wins[1, other]
    meet = jnp.maximum(jnp.minimum(hi_b, hi_o) - jnp.maximum(lo_b, lo_o), 0)
    num = jnp.where(live, meet + 16, 0)
    den = hi_b - lo_b + hi_o - lo_o + 16
    return b, o, num, den


def codes_of(rows, off):
    values = rows.astype(jnp.float32)
    row = lax.broadcasted_iota(jnp.int32, values.shape, 0)
    lane = lax.broadcasted_iota(jnp.int32, values.shape, 1)
    first = jnp.maximum(-off, 0) * CAP
    return [
        jnp.sum(
            jnp.where(jnp.logical_and(row == 0, lane == first + slot), values, 0.0)
        ).astype(jnp.int32)
        for slot in range(CAP)
    ]


def scale_of(num, den, samples):
    top = jnp.full((1, BS), num, jnp.int32).astype(jnp.float32)
    low = jnp.full((1, BS), den, jnp.int32).astype(jnp.float32)
    return top / low / samples


def at_block(index):
    return pl.ds(pl.multiple_of(index * BS, BS), BS)


def grams(scalars, off, codes, zown_ref, z_ref, tile_ref):
    samples = zown_ref.shape[1]
    found = [slot_of(*scalars, off, slot, codes[slot]) for slot in range(CAP)]
    for slot, (b, o, num, den) in enumerate(found):
        gram = lax.dot_general(
            zown_ref[at_block(b), :],
            z_ref[at_block(o), :],
            (((1,), (1,)), ((), ())),
            preferred_element_type=jnp.float32,
        )
        tile_ref[slot] = gram * scale_of(num, den, samples)
    return found


def products(found, zown_ref, z_ref, tile_ref, acc_ref, itself):
    width = acc_ref.shape[1]
    for slot, (b, o, _, _) in enumerate(found):
        tile = tile_ref[slot].astype(jnp.bfloat16)
        acc_ref[at_block(b), :] += jnp.dot(
            tile, z_ref[at_block(o), :width], preferred_element_type=jnp.float32
        )
        if itself:
            back = lax.dot_general(
                tile,
                zown_ref[at_block(b), :width],
                (((0,), (0,)), ((), ())),
                preferred_element_type=jnp.float32,
            )
            acc_ref[at_block(o), :] += back * jnp.where(b == o, 0.0, 1.0)


def put_tiles(ids, off, tile_ref, corr_ref, sem):
    mine = jnp.logical_and(off >= 0, lax.div(off, 2) == ids[1])
    first = jnp.where(jnp.logical_or(off == 1, off == 3), CAP, 0)
    copy = pltpu.make_async_copy(
        tile_ref, corr_ref.at[pl.ds(pl.multiple_of(first, CAP), CAP)], sem
    )

    @pl.when(mine)
    def _():
        copy.start()

    return mine, copy


def end_tiles(pending):
    mine, copy = pending

    @pl.when(mine)
    def _():
        copy.wait()


def self_kernel(ids, table, wins, own_ref, par_ref, zown_ref, acc_ref, corr_ref, tile_ref, sem):
    scalars = (ids, table, wins)
    width = own_ref.shape[1]
    normalise(lambda at: own_ref[at, :], lambda at: par_ref[at, :], zown_ref)
    found = grams(scalars, jnp.int32(0), [jnp.int32(-1)] * CAP, zown_ref, zown_ref, tile_ref)
    pending = put_tiles(ids, jnp.int32(0), tile_ref, corr_ref, sem)
    acc_ref[...] = zown_ref[:, :width].astype(jnp.float32)
    products(found, zown_ref, zown_ref, tile_ref, acc_ref, True)
    end_tiles(pending)


def either(first, one_ref, two_ref):
    return lambda at: jnp.where(first, one_ref[at, :], two_ref[at, :])


def plain(ref):
    return lambda at: ref[at, :]


def unit(scalars, off_of, own, par, table_ref, zown_ref, acc_ref, corr_ref, z_ref, tile_ref, sem):
    rows = zown_ref.shape[0]
    ids = scalars[0]
    off = off_of(lax.rem(ids[0], QUAD), ids[1])
    normalise(own, par, z_ref)
    codes = codes_of(table_ref[rows : rows + TABLE, :128], off)
    found = grams(scalars, off, codes, zown_ref, z_ref, tile_ref)
    pending = put_tiles(ids, off, tile_ref, corr_ref, sem)
    products(found, zown_ref, z_ref, tile_ref, acc_ref, False)
    return pending


def near_kernel(
    ids, table, wins, zown_ref, acc_in, own_ref, par_ref, _, acc_ref, corr_ref, z_ref, tile_ref, sem
):
    scalars = (ids, table, wins)
    width = acc_in.shape[1]
    acc_ref[:, :width] = acc_in[...]
    acc_ref[:, width:] = jnp.zeros_like(acc_in)
    refs = (zown_ref, acc_ref, corr_ref, z_ref, tile_ref, sem)
    end_tiles(unit(scalars, off_near, plain(own_ref), plain(par_ref), own_ref, *refs))


def next_kernel(
    ids, table, wins, zown_ref, acc_in, one_ref, two_ref, _, out_ref, give_ref, corr_ref, *scratch
):
    scalars = (ids, table, wins)
    acc_ref, z_ref, tile_ref, sem = scratch
    width = out_ref.shape[1]
    acc_ref[...] = acc_in[...]
    straight = lax.rem(ids[0], QUAD) != 0
    own, par = either(straight, one_ref, two_ref), either(straight, two_ref, one_ref)
    refs = (zown_ref, acc_ref, corr_ref, z_ref, tile_ref, sem)
    pending = unit(scalars, off_next, own, par, one_ref, *refs)
    out_ref[...] = acc_ref[:, :width]
    give_ref[...] = acc_ref[:, width:].astype(give_ref.dtype)
    end_tiles(pending)


def both_kernel(
    ids, table, wins, zown_ref, acc_in, own_ref, par_ref, _, out_ref, corr_ref, z_ref, tile_ref, sem
):
    scalars = (ids, table, wins)
    out_ref[...] = acc_in[...]
    refs = (zown_ref, out_ref, corr_ref, z_ref, tile_ref, sem)
    end_tiles(unit(scalars, off_zx, plain(own_ref), plain(par_ref), own_ref, *refs))


def last_kernel(
    ids, table, wins, zown_ref, acc_in, own_ref, par_ref, got_ref, _, out_ref, corr_ref, *scratch
):
    scalars = (ids, table, wins)
    acc_ref, z_ref, tile_ref, sem = scratch
    acc_ref[...] = acc_in[...] + got_ref[...].astype(jnp.float32)
    refs = (zown_ref, acc_ref, corr_ref, z_ref, tile_ref, sem)
    pending = unit(scalars, off_last, plain(own_ref), plain(par_ref), own_ref, *refs)
    out_ref[...] = acc_ref[...].astype(out_ref.dtype)
    end_tiles(pending)


def last_two_kernel(
    ids, table, wins, zown_ref, acc_in, zx_ref, zx_par, own_ref, par_ref, got_ref, _, out_ref, corr_ref, *scratch
):
    scalars = (ids, table, wins)
    acc_ref, z_ref, tile_ref, sems = scratch
    acc_ref[...] = acc_in[...] + got_ref[...].astype(jnp.float32)
    pending = []
    for k, (off_of, own, swapped) in enumerate(
        ((off_zx, zx_ref, zx_par), (off_last, own_ref, par_ref))
    ):
        refs = (zown_ref, acc_ref, corr_ref, z_ref.at[k], tile_ref.at[k], sems.at[k])
        pending.append(unit(scalars, off_of, plain(own), plain(swapped), own, *refs))
    out_ref[...] = acc_ref[...].astype(out_ref.dtype)
    for one in pending:
        end_tiles(one)


SMEM = pl.BlockSpec(memory_space=pltpu.SMEM)
INSIDE = pl.BlockSpec(memory_space=pltpu.VMEM)
ANY = pl.BlockSpec(memory_space=pl.ANY)


def estimate(mib):
    return pl.CostEstimate(flops=1, bytes_accessed=1 + int(mib * 2**20), transcendentals=0)


EST = {"last": 20, "near": 4, "next": 0, "self": 0, "zx_p": 8}


def run_self(ids, table, wins, own, par):
    rows, width = own.shape
    return pl.pallas_call(
        self_kernel,
        out_shape=(
            jax.ShapeDtypeStruct((rows, 2 * width), jnp.bfloat16),
            jax.ShapeDtypeStruct((rows, width), jnp.float32),
            jax.ShapeDtypeStruct((2 * CAP, BS, BS), jnp.float32),
        ),
        in_specs=[SMEM, SMEM, SMEM, INSIDE, INSIDE],
        out_specs=(INSIDE, INSIDE, ANY),
        scratch_shapes=[pltpu.VMEM((CAP, BS, BS), jnp.float32), pltpu.SemaphoreType.DMA],
        compiler_params=pltpu.CompilerParams(vmem_limit_bytes=VMEM),
        cost_estimate=estimate(EST["self"]),
        name="self_pairs",
    )(ids, table, wins, own, par)


def run_unit(kernel, name, corr, inputs, outs, acc_shape=None, units=None):
    rows, both = inputs[3].shape
    many = (units,) if units else ()
    scratch = [pltpu.VMEM(acc_shape, jnp.float32)] if acc_shape else []
    outs = [jax.ShapeDtypeStruct((rows, width), dtype) for width, dtype in outs]
    return pl.pallas_call(
        kernel,
        out_shape=(*outs, jax.ShapeDtypeStruct(corr.shape, corr.dtype)),
        in_specs=[SMEM] * 3 + [INSIDE] * (len(inputs) - 3) + [ANY],
        out_specs=(*[INSIDE] * len(outs), ANY),
        scratch_shapes=scratch
        + [
            pltpu.VMEM((*many, rows, both), jnp.bfloat16),
            pltpu.VMEM((*many, CAP, BS, BS), jnp.float32),
            pltpu.SemaphoreType.DMA(many),
        ],
        input_output_aliases={len(inputs): len(outs)},
        compiler_params=pltpu.CompilerParams(vmem_limit_bytes=VMEM),
        cost_estimate=estimate(EST[name[:4]]),
        name=name,
    )(*inputs, corr)


def with_table(spectra, table, position):
    rows, width = spectra.shape
    first = table[:1] - position * BLK_DEV
    group = lax.broadcasted_iota(jnp.int32, first.shape, 1) // CAP
    second = table[1:] - (position + group) * BLK_DEV
    code = jnp.where(table[:1] >= 0, first * BLK_DEV + second, -1).astype(spectra.dtype)
    code = jnp.pad(code, ((rows, TABLE - 1), (0, width - code.shape[1])))
    return jnp.pad(spectra, ((0, TABLE), (0, 0))) + code


def body(spectra, pair_blocks, windows):
    hold = lax.optimization_barrier
    position = lax.axis_index("feat")
    rows, width = spectra.shape
    both = 2 * width
    par = swap(spectra)
    table, wins = pair_blocks.T, windows.T
    unit = with_table(spectra, table, position)
    near_own = send(unit, move_near)
    from_z = send(unit, move_z)
    near_par = send(par, move_near)
    ids = jnp.stack([position, lax.axis_index("samp")]).astype(jnp.int32)
    scalars = (ids, table, wins)
    zown, acc, corr = run_self(ids, table, wins, spectra, par)
    near_own, acc = hold((near_own, acc))
    next_own = send(near_own, move_next)
    from_z, acc = hold((from_z, acc))
    zx = send(from_z, move_x)
    near_par, _ = hold((near_par, acc))
    next_par = send(near_par, move_next)
    next_own, next_par, acc = hold((next_own, next_par, acc))
    acc, corr = run_unit(
        near_kernel,
        "near_pairs",
        corr,
        (*scalars, zown, acc, near_own, near_par),
        [(both, jnp.float32)],
    )
    next_own, near_par = hold((next_own, near_par))
    last = send(next_own, move_last)
    acc, give, corr = run_unit(
        next_kernel,
        "next_pairs",
        corr,
        (*scalars, zown, acc, next_own, next_par),
        [(width, jnp.float32), (width, jnp.bfloat16)],
        (rows, both),
    )
    zx, acc = hold((zx, acc))
    acc, corr = run_unit(
        both_kernel,
        "zx_pairs",
        corr,
        (*scalars, zown, acc, zx, swap(zx)),
        [(width, jnp.float32)],
    )
    profiles, corr = run_unit(
        last_kernel,
        "last_pairs",
        corr,
        (*scalars, zown, acc, last, swap(last), swap(give)),
        [(width, jnp.bfloat16)],
        (rows, width),
    )
    return (corr, profiles)


def solution(mesh):
    placed = (P("feat", "samp"), P("feat", None), P())
    return jax.shard_map(
        body,
        mesh=mesh,
        in_specs=placed,
        out_specs=(P(("feat", "samp"), None, None), P("feat", "samp")),
        check_vma=False,
    )
```

```python
import functools

import jax
import jax.numpy as jnp
from jax import lax
from jax.experimental import pallas as pl
from jax.experimental.pallas import tpu as pltpu
from jax.sharding import PartitionSpec as P

BS = 256
BLK_DEV = 4
CAP = 8
REACH = 3
SLOTS = (REACH + 1) * CAP
QUAD = 4
EPS = 1e-05
STEP = 256
TABLE = 2 * CAP
PARTS = 2
VMEM = 24 * 1024 * 1024


def along_x(i):
    return i ^ 1


def along_y(i):
    return i ^ 2


def along_z_side(i, n):
    return (i + QUAD if i % QUAD < 2 else i - QUAD) % n


def move_near(i, core, n):
    return (along_x(i), 0) if core == 0 else (along_y(i), 1)


def move_z(i, core, n):
    return (i - QUAD if i % 2 == 0 else i + QUAD) % n, core


def move_next(i, core, n):
    if core == 0:
        to = along_y(i)
        return to, (1 if to % QUAD == 0 else 0)
    to = along_z_side(i, n)
    return to, (0 if to % QUAD == 0 else 1)


def move_x(i, core, n):
    return along_x(i), core


def move_last(i, core, n):
    holds_diag = core == (1 if i % QUAD == 0 else 0)
    return (along_z_side(i, n), 0) if holds_diag else (along_x(i), 1)


def send(value, move):
    length, cores = lax.axis_size("feat"), lax.axis_size("samp")
    pairs = []
    for i in range(length):
        for core in range(cores):
            to, to_core = move(i, core, length)
            pairs.append((i * cores + core, to * cores + to_core))
    return lax.ppermute(value, ("feat", "samp"), pairs)


def swap(value):
    return lax.ppermute(value, "samp", [(0, 1), (1, 0)])


def off_near(r, core):
    return jnp.where(core == 0, 1 - 2 * lax.rem(r, 2), 2 - 4 * lax.div(r, 2))


def off_next(r, core):
    return jnp.where((core == 0) != (r == 0), 3 - 2 * r, 4 * lax.div(r, 2) - 2)


def off_zx(r, core):
    return 6 * lax.rem(r, 2) - 3


def off_last(r, core):
    return jnp.where(r == 0, -1, jnp.where(r == 1, -3, jnp.where(r == 2, 3, 1)))


def normalise(read_own, read_par, z_ref):
    rows = z_ref.shape[0]
    width = z_ref.shape[1] // 2
    total = 2 * width
    for at in range(0, rows, STEP):
        here = slice(at, at + STEP)
        a = read_own(here).astype(jnp.float32)
        b = read_par(here).astype(jnp.float32)
        mean = jnp.sum(a + b, axis=1, keepdims=True) / total
        var = jnp.sum(a * a + b * b, axis=1, keepdims=True) / total - mean * mean
        inv = lax.rsqrt(var + EPS)
        z_ref[here, :width] = ((a - mean) * inv).astype(jnp.bfloat16)
        z_ref[here, width:] = ((b - mean) * inv).astype(jnp.bfloat16)


def slot_of(ids, table, wins, off, slot, code):
    position = ids[0]
    ahead = off >= 0
    at = jnp.maximum(off, 0) * CAP + slot
    left = jnp.where(ahead, table[0, at] - position * BLK_DEV, lax.div(code, BLK_DEV))
    right = jnp.where(ahead, table[1, at] - (position + off) * BLK_DEV, lax.rem(code, BLK_DEV))
    live = jnp.where(ahead, table[0, at], code) >= 0
    live = jnp.logical_and(live, position + off >= 0)
    b = jnp.where(live, jnp.where(ahead, left, right), 0)
    o = jnp.where(live, jnp.where(ahead, right, left), 0)
    mine = position * BLK_DEV + b
    other = jnp.where(live, (position + off) * BLK_DEV + o, 0)
    lo_b, hi_b = wins[0, mine], wins[1, mine]
    lo_o, hi_o = wins[0, other], wins[1, other]
    meet = jnp.maximum(jnp.minimum(hi_b, hi_o) - jnp.maximum(lo_b, lo_o), 0)
    num = jnp.where(live, meet + 16, 0)
    den = hi_b - lo_b + hi_o - lo_o + 16
    return b, o, num, den


def codes_of(rows, off):
    values = rows.astype(jnp.float32)
    row = lax.broadcasted_iota(jnp.int32, values.shape, 0)
    lane = lax.broadcasted_iota(jnp.int32, values.shape, 1)
    first = jnp.maximum(-off, 0) * CAP
    return [
        jnp.sum(
            jnp.where(jnp.logical_and(row == 0, lane == first + slot), values, 0.0)
        ).astype(jnp.int32)
        for slot in range(CAP)
    ]


def scale_of(num, den, samples):
    top = jnp.full((1, BS), num, jnp.int32).astype(jnp.float32)
    low = jnp.full((1, BS), den, jnp.int32).astype(jnp.float32)
    return top / low / samples


def at_block(index):
    return pl.ds(pl.multiple_of(index * BS, BS), BS)


def grams(found, zown_ref, z_ref, tile_ref):
    samples = zown_ref.shape[1]
    for slot, (b, o, num, den) in found:
        gram = lax.dot_general(
            zown_ref[at_block(b), :],
            z_ref[at_block(o), :],
            (((1,), (1,)), ((), ())),
            preferred_element_type=jnp.float32,
        )
        tile_ref[slot] = gram * scale_of(num, den, samples)


def products(found, zown_ref, z_ref, tile_ref, acc_ref, itself):
    width = acc_ref.shape[1]
    for slot, (b, o, _, _) in found:
        tile = tile_ref[slot].astype(jnp.bfloat16)
        acc_ref[at_block(b), :] += jnp.dot(
            tile, z_ref[at_block(o), :width], preferred_element_type=jnp.float32
        )
        if itself:
            back = lax.dot_general(
                tile,
                zown_ref[at_block(b), :width],
                (((0,), (0,)), ((), ())),
                preferred_element_type=jnp.float32,
            )
            acc_ref[at_block(o), :] += back * jnp.where(b == o, 0.0, 1.0)


def put_tiles(ids, off, some, tile_ref, corr_ref, sem):
    mine = jnp.logical_and(off >= 0, lax.div(off, 2) == ids[1])
    first = jnp.where(jnp.logical_or(off == 1, off == 3), CAP, 0) + some.start
    copy = pltpu.make_async_copy(
        tile_ref.at[some], corr_ref.at[pl.ds(first, some.stop - some.start)], sem
    )

    @pl.when(mine)
    def _():
        copy.start()

    return mine, copy


def end_tiles(pending):
    for mine, copy in pending:

        @pl.when(mine)
        def _(copy=copy):
            copy.wait()


def grams_out(scalars, off, codes, zown_ref, z_ref, tile_ref, corr_ref, sems):
    found = [(slot, slot_of(*scalars, off, slot, codes[slot])) for slot in range(CAP)]
    pending = []
    for part in range(PARTS):
        some = slice(part * CAP // PARTS, (part + 1) * CAP // PARTS)
        grams(found[some], zown_ref, z_ref, tile_ref)
        pending.append(put_tiles(scalars[0], off, some, tile_ref, corr_ref, sems.at[part]))
    return found, pending


def self_kernel(ids, table, wins, own_ref, par_ref, zown_ref, acc_ref, corr_ref, tile_ref, sems):
    scalars = (ids, table, wins)
    width = own_ref.shape[1]
    normalise(lambda at: own_ref[at, :], lambda at: par_ref[at, :], zown_ref)
    none = [jnp.int32(-1)] * CAP
    found, pending = grams_out(
        scalars, jnp.int32(0), none, zown_ref, zown_ref, tile_ref, corr_ref, sems
    )
    acc_ref[...] = zown_ref[:, :width].astype(jnp.float32)
    products(found, zown_ref, zown_ref, tile_ref, acc_ref, True)
    end_tiles(pending)


def either(first, one_ref, two_ref):
    return lambda at: jnp.where(first, one_ref[at, :], two_ref[at, :])


def plain(ref):
    return lambda at: ref[at, :]


def unit(scalars, off_of, own, par, table_ref, zown_ref, acc_ref, corr_ref, z_ref, tile_ref, sem):
    rows = zown_ref.shape[0]
    ids = scalars[0]
    off = off_of(lax.rem(ids[0], QUAD), ids[1])
    normalise(own, par, z_ref)
    codes = codes_of(table_ref[rows : rows + TABLE, :128], off)
    found, pending = grams_out(scalars, off, codes, zown_ref, z_ref, tile_ref, corr_ref, sem)
    products(found, zown_ref, z_ref, tile_ref, acc_ref, False)
    return pending


def near_kernel(
    ids, table, wins, zown_ref, acc_in, own_ref, par_ref, _, acc_ref, corr_ref, z_ref, tile_ref, sem
):
    scalars = (ids, table, wins)
    width = acc_in.shape[1]
    acc_ref[:, :width] = acc_in[...]
    acc_ref[:, width:] = jnp.zeros_like(acc_in)
    refs = (zown_ref, acc_ref, corr_ref, z_ref, tile_ref, sem)
    end_tiles(unit(scalars, off_near, plain(own_ref), plain(par_ref), own_ref, *refs))


def next_kernel(
    ids, table, wins, zown_ref, acc_in, one_ref, two_ref, _, out_ref, give_ref, corr_ref, *scratch
):
    scalars = (ids, table, wins)
    acc_ref, z_ref, tile_ref, sem = scratch
    width = out_ref.shape[1]
    acc_ref[...] = acc_in[...]
    straight = lax.rem(ids[0], QUAD) != 0
    own, par = either(straight, one_ref, two_ref), either(straight, two_ref, one_ref)
    refs = (zown_ref, acc_ref, corr_ref, z_ref, tile_ref, sem)
    pending = unit(scalars, off_next, own, par, one_ref, *refs)
    out_ref[...] = acc_ref[:, :width]
    give_ref[...] = acc_ref[:, width:].astype(give_ref.dtype)
    end_tiles(pending)


def both_kernel(
    ids, table, wins, zown_ref, acc_in, own_ref, par_ref, _, out_ref, corr_ref, z_ref, tile_ref, sem
):
    scalars = (ids, table, wins)
    out_ref[...] = acc_in[...]
    refs = (zown_ref, out_ref, corr_ref, z_ref, tile_ref, sem)
    end_tiles(unit(scalars, off_zx, plain(own_ref), plain(par_ref), own_ref, *refs))


def last_kernel(
    ids, table, wins, zown_ref, acc_in, own_ref, par_ref, got_ref, _, out_ref, corr_ref, *scratch
):
    scalars = (ids, table, wins)
    acc_ref, z_ref, tile_ref, sem = scratch
    acc_ref[...] = acc_in[...] + got_ref[...].astype(jnp.float32)
    refs = (zown_ref, acc_ref, corr_ref, z_ref, tile_ref, sem)
    pending = unit(scalars, off_last, plain(own_ref), plain(par_ref), own_ref, *refs)
    out_ref[...] = acc_ref[...].astype(out_ref.dtype)
    end_tiles(pending)


def last_two_kernel(
    ids, table, wins, zown_ref, acc_in, zx_ref, zx_par, own_ref, par_ref, got_ref, _, out_ref, corr_ref, *scratch
):
    scalars = (ids, table, wins)
    acc_ref, z_ref, tile_ref, sems = scratch
    acc_ref[...] = acc_in[...] + got_ref[...].astype(jnp.float32)
    pending = []
    for k, (off_of, own, swapped) in enumerate(
        ((off_zx, zx_ref, zx_par), (off_last, own_ref, par_ref))
    ):
        refs = (zown_ref, acc_ref, corr_ref, z_ref.at[k], tile_ref.at[k], sems.at[k])
        pending.append(unit(scalars, off_of, plain(own), plain(swapped), own, *refs))
    out_ref[...] = acc_ref[...].astype(out_ref.dtype)
    for one in pending:
        end_tiles(one)


SMEM = pl.BlockSpec(memory_space=pltpu.SMEM)
INSIDE = pl.BlockSpec(memory_space=pltpu.VMEM)
ANY = pl.BlockSpec(memory_space=pl.ANY)


def estimate(mib):
    return pl.CostEstimate(flops=1, bytes_accessed=1 + int(mib * 2**20), transcendentals=0)


EST = {"last": 4, "near": 0.5, "next": 0, "self": 2, "zx_p": 60}


def run_self(ids, table, wins, own, par):
    rows, width = own.shape
    return pl.pallas_call(
        self_kernel,
        out_shape=(
            jax.ShapeDtypeStruct((rows, 2 * width), jnp.bfloat16),
            jax.ShapeDtypeStruct((rows, width), jnp.float32),
            jax.ShapeDtypeStruct((2 * CAP, BS, BS), jnp.float32),
        ),
        in_specs=[SMEM, SMEM, SMEM, INSIDE, INSIDE],
        out_specs=(INSIDE, INSIDE, ANY),
        scratch_shapes=[pltpu.VMEM((CAP, BS, BS), jnp.float32), pltpu.SemaphoreType.DMA((PARTS,))],
        compiler_params=pltpu.CompilerParams(vmem_limit_bytes=VMEM),
        cost_estimate=estimate(EST["self"]),
        name="self_pairs",
    )(ids, table, wins, own, par)


def run_unit(kernel, name, corr, inputs, outs, acc_shape=None, units=None):
    rows, both = inputs[3].shape
    many = (units,) if units else ()
    scratch = [pltpu.VMEM(acc_shape, jnp.float32)] if acc_shape else []
    outs = [jax.ShapeDtypeStruct((rows, width), dtype) for width, dtype in outs]
    return pl.pallas_call(
        kernel,
        out_shape=(*outs, jax.ShapeDtypeStruct(corr.shape, corr.dtype)),
        in_specs=[SMEM] * 3 + [INSIDE] * (len(inputs) - 3) + [ANY],
        out_specs=(*[INSIDE] * len(outs), ANY),
        scratch_shapes=scratch
        + [
            pltpu.VMEM((*many, rows, both), jnp.bfloat16),
            pltpu.VMEM((*many, CAP, BS, BS), jnp.float32),
            pltpu.SemaphoreType.DMA((*many, PARTS)),
        ],
        input_output_aliases={len(inputs): len(outs)},
        compiler_params=pltpu.CompilerParams(vmem_limit_bytes=VMEM),
        cost_estimate=estimate(EST[name[:4]]),
        name=name,
    )(*inputs, corr)


def with_table(spectra, table, position):
    rows, width = spectra.shape
    first = table[:1] - position * BLK_DEV
    group = lax.broadcasted_iota(jnp.int32, first.shape, 1) // CAP
    second = table[1:] - (position + group) * BLK_DEV
    code = jnp.where(table[:1] >= 0, first * BLK_DEV + second, -1).astype(spectra.dtype)
    code = jnp.pad(code, ((rows, TABLE - 1), (0, width - code.shape[1])))
    return jnp.pad(spectra, ((0, TABLE), (0, 0))) + code


def body(spectra, pair_blocks, windows):
    hold = lax.optimization_barrier
    position = lax.axis_index("feat")
    rows, width = spectra.shape
    both = 2 * width
    table, wins = pair_blocks.T, windows.T
    unit = with_table(spectra, table, position)
    par = swap(unit)
    near_own = send(unit, move_near)
    from_z = send(unit, move_z)
    near_par = send(par, move_near)
    ids = jnp.stack([position, lax.axis_index("samp")]).astype(jnp.int32)
    scalars = (ids, table, wins)
    zown, acc, corr = run_self(ids, table, wins, spectra, par)
    near_own, _ = hold((near_own, acc))
    next_own = send(near_own, move_next)
    from_z, _ = hold((from_z, acc))
    zx = send(from_z, move_x)
    next_par = send(near_par, move_next)
    acc, corr = run_unit(
        near_kernel,
        "near_pairs",
        corr,
        (*scalars, zown, acc, near_own, near_par),
        [(both, jnp.float32)],
    )
    next_own, _ = hold((next_own, acc))
    last = send(next_own, move_last)
    next_par, acc = hold((next_par, acc))
    acc, give, corr = run_unit(
        next_kernel,
        "next_pairs",
        corr,
        (*scalars, zown, acc, next_own, next_par),
        [(width, jnp.float32), (width, jnp.bfloat16)],
        (rows, both),
    )
    zx, acc = hold((zx, acc))
    got = swap(give)
    acc, corr = run_unit(
        both_kernel,
        "zx_pairs",
        corr,
        (*scalars, zown, acc, zx, swap(zx)),
        [(width, jnp.float32)],
    )
    profiles, corr = run_unit(
        last_kernel,
        "last_pairs",
        corr,
        (*scalars, zown, acc, last, swap(last), got),
        [(width, jnp.bfloat16)],
        (rows, width),
    )
    return (corr, profiles)


def solution(mesh):
    placed = (P("feat", "samp"), P("feat", None), P())
    return jax.shard_map(
        body,
        mesh=mesh,
        in_specs=placed,
        out_specs=(P(("feat", "samp"), None, None), P("feat", "samp")),
        check_vma=False,
    )
```

```python
import functools

import jax
import jax.numpy as jnp
from jax import lax
from jax.experimental import pallas as pl
from jax.experimental.pallas import tpu as pltpu
from jax.sharding import PartitionSpec as P

BS = 256
BLK_DEV = 4
CAP = 8
REACH = 3
SLOTS = (REACH + 1) * CAP
QUAD = 4
EPS = 1e-05
STEP = 256
TABLE = 2 * CAP
PARTS = 2
VMEM = 24 * 1024 * 1024


def along_x(i):
    return i ^ 1


def along_y(i):
    return i ^ 2


def along_z_side(i, n):
    return (i + QUAD if i % QUAD < 2 else i - QUAD) % n


def move_near(i, core, n):
    return (along_x(i), 0) if core == 0 else (along_y(i), 1)


def move_z(i, core, n):
    return (i - QUAD if i % 2 == 0 else i + QUAD) % n, core


def move_next(i, core, n):
    if core == 0:
        to = along_y(i)
        return to, (1 if to % QUAD == 0 else 0)
    to = along_z_side(i, n)
    return to, (0 if to % QUAD == 0 else 1)


def move_x(i, core, n):
    return along_x(i), core


def move_last(i, core, n):
    holds_diag = core == (1 if i % QUAD == 0 else 0)
    return (along_z_side(i, n), 0) if holds_diag else (along_x(i), 1)


def send(value, move):
    length, cores = lax.axis_size("feat"), lax.axis_size("samp")
    pairs = []
    for i in range(length):
        for core in range(cores):
            to, to_core = move(i, core, length)
            pairs.append((i * cores + core, to * cores + to_core))
    return lax.ppermute(value, ("feat", "samp"), pairs)


def swap(value):
    return lax.ppermute(value, "samp", [(0, 1), (1, 0)])


def off_near(r, core):
    return jnp.where(core == 0, 1 - 2 * lax.rem(r, 2), 2 - 4 * lax.div(r, 2))


def off_next(r, core):
    return jnp.where((core == 0) != (r == 0), 3 - 2 * r, 4 * lax.div(r, 2) - 2)


def off_zx(r, core):
    return 6 * lax.rem(r, 2) - 3


def off_last(r, core):
    return jnp.where(r == 0, -1, jnp.where(r == 1, -3, jnp.where(r == 2, 3, 1)))


def normalise(read_own, read_par, z_ref):
    rows = z_ref.shape[0]
    width = z_ref.shape[1] // 2
    total = 2 * width
    for at in range(0, rows, STEP):
        here = slice(at, at + STEP)
        a = read_own(here).astype(jnp.float32)
        b = read_par(here).astype(jnp.float32)
        mean = jnp.sum(a + b, axis=1, keepdims=True) / total
        var = jnp.sum(a * a + b * b, axis=1, keepdims=True) / total - mean * mean
        inv = lax.rsqrt(var + EPS)
        z_ref[here, :width] = ((a - mean) * inv).astype(jnp.bfloat16)
        z_ref[here, width:] = ((b - mean) * inv).astype(jnp.bfloat16)


def slot_of(ids, table, wins, off, slot, code):
    position = ids[0]
    ahead = off >= 0
    at = jnp.maximum(off, 0) * CAP + slot
    left = jnp.where(ahead, table[0, at] - position * BLK_DEV, lax.div(code, BLK_DEV))
    right = jnp.where(ahead, table[1, at] - (position + off) * BLK_DEV, lax.rem(code, BLK_DEV))
    live = jnp.where(ahead, table[0, at], code) >= 0
    live = jnp.logical_and(live, position + off >= 0)
    b = jnp.where(live, jnp.where(ahead, left, right), 0)
    o = jnp.where(live, jnp.where(ahead, right, left), 0)
    mine = position * BLK_DEV + b
    other = jnp.where(live, (position + off) * BLK_DEV + o, 0)
    lo_b, hi_b = wins[0, mine], wins[1, mine]
    lo_o, hi_o = wins[0, other], wins[1, other]
    meet = jnp.maximum(jnp.minimum(hi_b, hi_o) - jnp.maximum(lo_b, lo_o), 0)
    num = jnp.where(live, meet + 16, 0)
    den = hi_b - lo_b + hi_o - lo_o + 16
    return b, o, num, den


def codes_of(rows, off):
    values = rows.astype(jnp.float32)
    row = lax.broadcasted_iota(jnp.int32, values.shape, 0)
    values = jnp.where(row == 0, BLK_DEV * values, values)
    lane = lax.broadcasted_iota(jnp.int32, values.shape, 1)
    first = jnp.maximum(-off, 0) * CAP
    return [
        jnp.sum(
            jnp.where(jnp.logical_and(row < 2, lane == first + slot), values, 0.0)
        ).astype(jnp.int32)
        for slot in range(CAP)
    ]


def scale_of(num, den, samples):
    top = jnp.full((1, BS), num, jnp.int32).astype(jnp.float32)
    low = jnp.full((1, BS), den, jnp.int32).astype(jnp.float32)
    return top / low / samples


def at_block(index):
    return pl.ds(pl.multiple_of(index * BS, BS), BS)


def grams(found, zown_ref, z_ref, tile_ref):
    samples = zown_ref.shape[1]
    for slot, (b, o, num, den) in found:
        gram = lax.dot_general(
            zown_ref[at_block(b), :],
            z_ref[at_block(o), :],
            (((1,), (1,)), ((), ())),
            preferred_element_type=jnp.float32,
        )
        tile_ref[slot] = gram * scale_of(num, den, samples)


def products(found, zown_ref, z_ref, tile_ref, acc_ref, itself):
    width = acc_ref.shape[1]
    for slot, (b, o, _, _) in found:
        tile = tile_ref[slot].astype(jnp.bfloat16)
        acc_ref[at_block(b), :] += jnp.dot(
            tile, z_ref[at_block(o), :width], preferred_element_type=jnp.float32
        )
        if itself:
            back = lax.dot_general(
                tile,
                zown_ref[at_block(b), :width],
                (((0,), (0,)), ((), ())),
                preferred_element_type=jnp.float32,
            )
            acc_ref[at_block(o), :] += back * jnp.where(b == o, 0.0, 1.0)


def put_tiles(ids, off, some, tile_ref, corr_ref, sem):
    mine = jnp.logical_and(off >= 0, lax.div(off, 2) == ids[1])
    first = jnp.where(jnp.logical_or(off == 1, off == 3), CAP, 0) + some.start
    copy = pltpu.make_async_copy(
        tile_ref.at[some], corr_ref.at[pl.ds(first, some.stop - some.start)], sem
    )

    @pl.when(mine)
    def _():
        copy.start()

    return mine, copy


def end_tiles(pending):
    for mine, copy in pending:

        @pl.when(mine)
        def _(copy=copy):
            copy.wait()


def grams_out(scalars, off, codes, zown_ref, z_ref, tile_ref, corr_ref, sems):
    found = [(slot, slot_of(*scalars, off, slot, codes[slot])) for slot in range(CAP)]
    pending = []
    for part in range(PARTS):
        some = slice(part * CAP // PARTS, (part + 1) * CAP // PARTS)
        grams(found[some], zown_ref, z_ref, tile_ref)
        pending.append(put_tiles(scalars[0], off, some, tile_ref, corr_ref, sems.at[part]))
    return found, pending


def self_kernel(ids, table, wins, own_ref, par_ref, zown_ref, acc_ref, corr_ref, tile_ref, sems):
    scalars = (ids, table, wins)
    width = own_ref.shape[1]
    normalise(lambda at: own_ref[at, :], lambda at: par_ref[at, :], zown_ref)
    none = [jnp.int32(-1)] * CAP
    found, pending = grams_out(
        scalars, jnp.int32(0), none, zown_ref, zown_ref, tile_ref, corr_ref, sems
    )
    acc_ref[...] = zown_ref[:, :width].astype(jnp.float32)
    products(found, zown_ref, zown_ref, tile_ref, acc_ref, True)
    end_tiles(pending)


def either(first, one_ref, two_ref):
    return lambda at: jnp.where(first, one_ref[at, :], two_ref[at, :])


def plain(ref):
    return lambda at: ref[at, :]


def unit(scalars, off_of, own, par, table_ref, zown_ref, acc_ref, corr_ref, z_ref, tile_ref, sem):
    rows = zown_ref.shape[0]
    ids = scalars[0]
    off = off_of(lax.rem(ids[0], QUAD), ids[1])
    normalise(own, par, z_ref)
    codes = codes_of(table_ref[rows : rows + TABLE, :128], off)
    found, pending = grams_out(scalars, off, codes, zown_ref, z_ref, tile_ref, corr_ref, sem)
    products(found, zown_ref, z_ref, tile_ref, acc_ref, False)
    return pending


def near_kernel(
    ids, table, wins, zown_ref, acc_in, own_ref, par_ref, _, acc_ref, corr_ref, z_ref, tile_ref, sem
):
    scalars = (ids, table, wins)
    width = acc_in.shape[1]
    acc_ref[:, :width] = acc_in[...]
    acc_ref[:, width:] = jnp.zeros_like(acc_in)
    refs = (zown_ref, acc_ref, corr_ref, z_ref, tile_ref, sem)
    end_tiles(unit(scalars, off_near, plain(own_ref), plain(par_ref), own_ref, *refs))


def next_kernel(
    ids, table, wins, zown_ref, acc_in, one_ref, two_ref, _, out_ref, give_ref, corr_ref, *scratch
):
    scalars = (ids, table, wins)
    acc_ref, z_ref, tile_ref, sem = scratch
    width = out_ref.shape[1]
    acc_ref[...] = acc_in[...]
    straight = lax.rem(ids[0], QUAD) != 0
    own, par = either(straight, one_ref, two_ref), either(straight, two_ref, one_ref)
    refs = (zown_ref, acc_ref, corr_ref, z_ref, tile_ref, sem)
    pending = unit(scalars, off_next, own, par, one_ref, *refs)
    out_ref[...] = acc_ref[:, :width]
    give_ref[...] = acc_ref[:, width:].astype(give_ref.dtype)
    end_tiles(pending)


def both_kernel(
    ids, table, wins, zown_ref, acc_in, own_ref, par_ref, _, out_ref, corr_ref, z_ref, tile_ref, sem
):
    scalars = (ids, table, wins)
    out_ref[...] = acc_in[...]
    refs = (zown_ref, out_ref, corr_ref, z_ref, tile_ref, sem)
    end_tiles(unit(scalars, off_zx, plain(own_ref), plain(par_ref), own_ref, *refs))


def last_kernel(
    ids, table, wins, zown_ref, acc_in, own_ref, par_ref, got_ref, _, out_ref, corr_ref, *scratch
):
    scalars = (ids, table, wins)
    acc_ref, z_ref, tile_ref, sem = scratch
    acc_ref[...] = acc_in[...] + got_ref[...].astype(jnp.float32)
    refs = (zown_ref, acc_ref, corr_ref, z_ref, tile_ref, sem)
    pending = unit(scalars, off_last, plain(own_ref), plain(par_ref), own_ref, *refs)
    out_ref[...] = acc_ref[...].astype(out_ref.dtype)
    end_tiles(pending)


def last_two_kernel(
    ids, table, wins, zown_ref, acc_in, zx_ref, zx_par, own_ref, par_ref, got_ref, _, out_ref, corr_ref, *scratch
):
    scalars = (ids, table, wins)
    acc_ref, z_ref, tile_ref, sems = scratch
    acc_ref[...] = acc_in[...] + got_ref[...].astype(jnp.float32)
    pending = []
    for k, (off_of, own, swapped) in enumerate(
        ((off_zx, zx_ref, zx_par), (off_last, own_ref, par_ref))
    ):
        refs = (zown_ref, acc_ref, corr_ref, z_ref.at[k], tile_ref.at[k], sems.at[k])
        pending.append(unit(scalars, off_of, plain(own), plain(swapped), own, *refs))
    out_ref[...] = acc_ref[...].astype(out_ref.dtype)
    for one in pending:
        end_tiles(one)


SMEM = pl.BlockSpec(memory_space=pltpu.SMEM)
INSIDE = pl.BlockSpec(memory_space=pltpu.VMEM)
ANY = pl.BlockSpec(memory_space=pl.ANY)


def estimate(mib):
    return pl.CostEstimate(flops=1, bytes_accessed=1 + int(mib * 2**20), transcendentals=0)


EST = {"last": 0, "near": 20, "next": 0.5, "self": 2, "zx_p": 60}


def run_self(ids, table, wins, own, par):
    rows, width = own.shape
    return pl.pallas_call(
        self_kernel,
        out_shape=(
            jax.ShapeDtypeStruct((rows, 2 * width), jnp.bfloat16),
            jax.ShapeDtypeStruct((rows, width), jnp.float32),
            jax.ShapeDtypeStruct((2 * CAP, BS, BS), jnp.float32),
        ),
        in_specs=[SMEM, SMEM, SMEM, INSIDE, INSIDE],
        out_specs=(INSIDE, INSIDE, ANY),
        scratch_shapes=[pltpu.VMEM((CAP, BS, BS), jnp.float32), pltpu.SemaphoreType.DMA((PARTS,))],
        compiler_params=pltpu.CompilerParams(vmem_limit_bytes=VMEM),
        cost_estimate=estimate(EST["self"]),
        name="self_pairs",
    )(ids, table, wins, own, par)


def run_unit(kernel, name, corr, inputs, outs, acc_shape=None, units=None):
    rows, both = inputs[3].shape
    many = (units,) if units else ()
    scratch = [pltpu.VMEM(acc_shape, jnp.float32)] if acc_shape else []
    outs = [jax.ShapeDtypeStruct((rows, width), dtype) for width, dtype in outs]
    return pl.pallas_call(
        kernel,
        out_shape=(*outs, jax.ShapeDtypeStruct(corr.shape, corr.dtype)),
        in_specs=[SMEM] * 3 + [INSIDE] * (len(inputs) - 3) + [ANY],
        out_specs=(*[INSIDE] * len(outs), ANY),
        scratch_shapes=scratch
        + [
            pltpu.VMEM((*many, rows, both), jnp.bfloat16),
            pltpu.VMEM((*many, CAP, BS, BS), jnp.float32),
            pltpu.SemaphoreType.DMA((*many, PARTS)),
        ],
        input_output_aliases={len(inputs): len(outs)},
        compiler_params=pltpu.CompilerParams(vmem_limit_bytes=VMEM),
        cost_estimate=estimate(EST[name[:4]]),
        name=name,
    )(*inputs, corr)


def with_table(spectra, table):
    rows, width = spectra.shape
    below = jnp.pad(table, ((rows, TABLE - 2), (0, width - table.shape[1])))
    below = jnp.where(below >= 0, lax.rem(below, BLK_DEV), -1).astype(spectra.dtype)
    return jnp.pad(spectra, ((0, TABLE), (0, 0))) + below


def body(spectra, pair_blocks, windows):
    hold = lax.optimization_barrier
    position = lax.axis_index("feat")
    rows, width = spectra.shape
    both = 2 * width
    table, wins = pair_blocks.T, windows.T
    unit = with_table(spectra, table)
    par = swap(unit)
    near_own = send(unit, move_near)
    from_z = send(unit, move_z)
    near_par = send(par, move_near)
    ids = jnp.stack([position, lax.axis_index("samp")]).astype(jnp.int32)
    scalars = (ids, table, wins)
    zown, acc, corr = run_self(ids, table, wins, spectra, par)
    from_z, _ = hold((from_z, acc))
    zx = send(from_z, move_x)
    near_par, acc = hold((near_par, acc))
    next_par = send(near_par, move_next)
    next_own = send(near_own, move_next)
    near_par, acc = hold((near_par, acc))
    acc, corr = run_unit(
        near_kernel,
        "near_pairs",
        corr,
        (*scalars, zown, acc, near_own, near_par),
        [(both, jnp.float32)],
    )
    next_own, _ = hold((next_own, acc))
    last = send(next_own, move_last)
    acc, give, corr = run_unit(
        next_kernel,
        "next_pairs",
        corr,
        (*scalars, zown, acc, next_own, next_par),
        [(width, jnp.float32), (width, jnp.bfloat16)],
        (rows, both),
    )
    zx, acc = hold((zx, acc))
    got = swap(give)
    acc, corr = run_unit(
        both_kernel,
        "zx_pairs",
        corr,
        (*scalars, zown, acc, zx, swap(zx)),
        [(width, jnp.float32)],
    )
    profiles, corr = run_unit(
        last_kernel,
        "last_pairs",
        corr,
        (*scalars, zown, acc, last, swap(last), got),
        [(width, jnp.bfloat16)],
        (rows, width),
    )
    return (corr, profiles)


def solution(mesh):
    placed = (P("feat", "samp"), P("feat", None), P())
    return jax.shard_map(
        body,
        mesh=mesh,
        in_specs=placed,
        out_specs=(P(("feat", "samp"), None, None), P("feat", "samp")),
        check_vma=False,
    )
```

```python
import functools

import jax
import jax.numpy as jnp
from jax import lax
from jax.experimental import pallas as pl
from jax.experimental.pallas import tpu as pltpu
from jax.sharding import PartitionSpec as P

BS = 256
BLK_DEV = 4
CAP = 8
REACH = 3
SLOTS = (REACH + 1) * CAP
QUAD = 4
EPS = 1e-05
STEP = 256
TABLE = 2 * CAP
PARTS = 2
VMEM = 24 * 1024 * 1024


def along_x(i):
    return i ^ 1


def along_y(i):
    return i ^ 2


def along_z_side(i, n):
    return (i + QUAD if i % QUAD < 2 else i - QUAD) % n


def move_near(i, core, n):
    return (along_x(i), 0) if core == 0 else (along_y(i), 1)


def move_z(i, core, n):
    return (i - QUAD if i % 2 == 0 else i + QUAD) % n, core


def move_next(i, core, n):
    if core == 0:
        to = along_y(i)
        return to, (1 if to % QUAD == 0 else 0)
    to = along_z_side(i, n)
    return to, (0 if to % QUAD == 0 else 1)


def move_x(i, core, n):
    return along_x(i), core


def move_last(i, core, n):
    holds_diag = core == (1 if i % QUAD == 0 else 0)
    return (along_z_side(i, n), 0) if holds_diag else (along_x(i), 1)


def send(value, move):
    length, cores = lax.axis_size("feat"), lax.axis_size("samp")
    pairs = []
    for i in range(length):
        for core in range(cores):
            to, to_core = move(i, core, length)
            pairs.append((i * cores + core, to * cores + to_core))
    return lax.ppermute(value, ("feat", "samp"), pairs)


def swap(value):
    return lax.ppermute(value, "samp", [(0, 1), (1, 0)])


def off_near(r, core):
    return jnp.where(core == 0, 1 - 2 * lax.rem(r, 2), 2 - 4 * lax.div(r, 2))


def off_next(r, core):
    return jnp.where((core == 0) != (r == 0), 3 - 2 * r, 4 * lax.div(r, 2) - 2)


def off_zx(r, core):
    return 6 * lax.rem(r, 2) - 3


def off_last(r, core):
    return jnp.where(r == 0, -1, jnp.where(r == 1, -3, jnp.where(r == 2, 3, 1)))


def normalise(read_own, read_par, z_ref):
    rows = z_ref.shape[0]
    width = z_ref.shape[1] // 2
    total = 2 * width
    for at in range(0, rows, STEP):
        here = slice(at, at + STEP)
        a = read_own(here).astype(jnp.float32)
        b = read_par(here).astype(jnp.float32)
        mean = jnp.sum(a + b, axis=1, keepdims=True) / total
        var = jnp.sum(a * a + b * b, axis=1, keepdims=True) / total - mean * mean
        inv = lax.rsqrt(var + EPS)
        z_ref[here, :width] = ((a - mean) * inv).astype(jnp.bfloat16)
        z_ref[here, width:] = ((b - mean) * inv).astype(jnp.bfloat16)


def slot_of(ids, table, wins, off, slot, code):
    position = ids[0]
    ahead = off >= 0
    at = jnp.maximum(off, 0) * CAP + slot
    left = jnp.where(ahead, table[0, at] - position * BLK_DEV, lax.div(code, BLK_DEV))
    right = jnp.where(ahead, table[1, at] - (position + off) * BLK_DEV, lax.rem(code, BLK_DEV))
    live = jnp.where(ahead, table[0, at], code) >= 0
    live = jnp.logical_and(live, position + off >= 0)
    b = jnp.where(live, jnp.where(ahead, left, right), 0)
    o = jnp.where(live, jnp.where(ahead, right, left), 0)
    mine = position * BLK_DEV + b
    other = jnp.where(live, (position + off) * BLK_DEV + o, 0)
    lo_b, hi_b = wins[0, mine], wins[1, mine]
    lo_o, hi_o = wins[0, other], wins[1, other]
    meet = jnp.maximum(jnp.minimum(hi_b, hi_o) - jnp.maximum(lo_b, lo_o), 0)
    num = jnp.where(live, meet + 16, 0)
    den = hi_b - lo_b + hi_o - lo_o + 16
    return b, o, num, den


def codes_of(rows, off):
    values = rows.astype(jnp.float32)
    row = lax.broadcasted_iota(jnp.int32, values.shape, 0)
    values = jnp.where(row == 0, BLK_DEV * values, values)
    lane = lax.broadcasted_iota(jnp.int32, values.shape, 1)
    first = jnp.maximum(-off, 0) * CAP
    return [
        jnp.sum(
            jnp.where(jnp.logical_and(row < 2, lane == first + slot), values, 0.0)
        ).astype(jnp.int32)
        for slot in range(CAP)
    ]


def scale_of(num, den, samples):
    top = jnp.full((1, BS), num, jnp.int32).astype(jnp.float32)
    low = jnp.full((1, BS), den, jnp.int32).astype(jnp.float32)
    return top / low / samples


def at_block(index):
    return pl.ds(pl.multiple_of(index * BS, BS), BS)


def grams(found, zown_ref, z_ref, tile_ref):
    samples = zown_ref.shape[1]
    for slot, (b, o, num, den) in found:
        gram = lax.dot_general(
            zown_ref[at_block(b), :],
            z_ref[at_block(o), :],
            (((1,), (1,)), ((), ())),
            preferred_element_type=jnp.float32,
        )
        tile_ref[slot] = gram * scale_of(num, den, samples)


def products(found, zown_ref, z_ref, tile_ref, acc_ref, itself):
    width = acc_ref.shape[1]
    for slot, (b, o, _, _) in found:
        tile = tile_ref[slot].astype(jnp.bfloat16)
        acc_ref[at_block(b), :] += jnp.dot(
            tile, z_ref[at_block(o), :width], preferred_element_type=jnp.float32
        )
        if itself:
            back = lax.dot_general(
                tile,
                zown_ref[at_block(b), :width],
                (((0,), (0,)), ((), ())),
                preferred_element_type=jnp.float32,
            )
            acc_ref[at_block(o), :] += back * jnp.where(b == o, 0.0, 1.0)


def put_tiles(ids, off, some, tile_ref, corr_ref, sem):
    mine = jnp.logical_and(off >= 0, lax.div(off, 2) == ids[1])
    first = jnp.where(jnp.logical_or(off == 1, off == 3), CAP, 0) + some.start
    copy = pltpu.make_async_copy(
        tile_ref.at[some], corr_ref.at[pl.ds(first, some.stop - some.start)], sem
    )

    @pl.when(mine)
    def _():
        copy.start()

    return mine, copy


def end_tiles(pending):
    for mine, copy in pending:

        @pl.when(mine)
        def _(copy=copy):
            copy.wait()


def grams_out(scalars, off, codes, zown_ref, z_ref, tile_ref, corr_ref, sems):
    found = [(slot, slot_of(*scalars, off, slot, codes[slot])) for slot in range(CAP)]
    pending = []
    for part in range(PARTS):
        some = slice(part * CAP // PARTS, (part + 1) * CAP // PARTS)
        grams(found[some], zown_ref, z_ref, tile_ref)
        pending.append(put_tiles(scalars[0], off, some, tile_ref, corr_ref, sems.at[part]))
    return found, pending


def self_kernel(ids, table, wins, own_ref, par_ref, zown_ref, acc_ref, corr_ref, tile_ref, sems):
    scalars = (ids, table, wins)
    width = own_ref.shape[1]
    normalise(lambda at: own_ref[at, :], lambda at: par_ref[at, :], zown_ref)
    none = [jnp.int32(-1)] * CAP
    found, pending = grams_out(
        scalars, jnp.int32(0), none, zown_ref, zown_ref, tile_ref, corr_ref, sems
    )
    acc_ref[...] = zown_ref[:, :width].astype(jnp.float32)
    products(found, zown_ref, zown_ref, tile_ref, acc_ref, True)
    end_tiles(pending)


def either(first, one_ref, two_ref):
    return lambda at: jnp.where(first, one_ref[at, :], two_ref[at, :])


def plain(ref):
    return lambda at: ref[at, :]


def unit(scalars, off_of, own, par, table_ref, zown_ref, acc_ref, corr_ref, z_ref, tile_ref, sem):
    rows = zown_ref.shape[0]
    ids = scalars[0]
    off = off_of(lax.rem(ids[0], QUAD), ids[1])
    normalise(own, par, z_ref)
    codes = codes_of(table_ref[rows : rows + TABLE, :128], off)
    found, pending = grams_out(scalars, off, codes, zown_ref, z_ref, tile_ref, corr_ref, sem)
    products(found, zown_ref, z_ref, tile_ref, acc_ref, False)
    return pending


def near_kernel(
    ids, table, wins, zown_ref, acc_in, own_ref, par_ref, _, acc_ref, corr_ref, z_ref, tile_ref, sem
):
    scalars = (ids, table, wins)
    width = acc_in.shape[1]
    acc_ref[:, :width] = acc_in[...]
    acc_ref[:, width:] = jnp.zeros_like(acc_in)
    refs = (zown_ref, acc_ref, corr_ref, z_ref, tile_ref, sem)
    end_tiles(unit(scalars, off_near, plain(own_ref), plain(par_ref), own_ref, *refs))


def next_kernel(
    ids, table, wins, zown_ref, acc_in, one_ref, two_ref, _, out_ref, give_ref, corr_ref, *scratch
):
    scalars = (ids, table, wins)
    acc_ref, z_ref, tile_ref, sem = scratch
    width = out_ref.shape[1]
    acc_ref[...] = acc_in[...]
    straight = lax.rem(ids[0], QUAD) != 0
    own, par = either(straight, one_ref, two_ref), either(straight, two_ref, one_ref)
    refs = (zown_ref, acc_ref, corr_ref, z_ref, tile_ref, sem)
    pending = unit(scalars, off_next, own, par, one_ref, *refs)
    out_ref[...] = acc_ref[:, :width]
    give_ref[...] = acc_ref[:, width:].astype(give_ref.dtype)
    end_tiles(pending)


def both_kernel(
    ids, table, wins, zown_ref, acc_in, own_ref, par_ref, _, out_ref, corr_ref, z_ref, tile_ref, sem
):
    scalars = (ids, table, wins)
    out_ref[...] = acc_in[...]
    refs = (zown_ref, out_ref, corr_ref, z_ref, tile_ref, sem)
    end_tiles(unit(scalars, off_zx, plain(own_ref), plain(par_ref), own_ref, *refs))


def last_kernel(
    ids, table, wins, zown_ref, acc_in, own_ref, par_ref, got_ref, _, out_ref, corr_ref, *scratch
):
    scalars = (ids, table, wins)
    acc_ref, z_ref, tile_ref, sem = scratch
    acc_ref[...] = acc_in[...] + got_ref[...].astype(jnp.float32)
    refs = (zown_ref, acc_ref, corr_ref, z_ref, tile_ref, sem)
    pending = unit(scalars, off_last, plain(own_ref), plain(par_ref), own_ref, *refs)
    out_ref[...] = acc_ref[...].astype(out_ref.dtype)
    end_tiles(pending)


def last_two_kernel(
    ids, table, wins, zown_ref, acc_in, zx_ref, zx_par, own_ref, par_ref, got_ref, _, out_ref, corr_ref, *scratch
):
    scalars = (ids, table, wins)
    acc_ref, z_ref, tile_ref, sems = scratch
    acc_ref[...] = acc_in[...] + got_ref[...].astype(jnp.float32)
    pending = []
    for k, (off_of, own, swapped) in enumerate(
        ((off_zx, zx_ref, zx_par), (off_last, own_ref, par_ref))
    ):
        refs = (zown_ref, acc_ref, corr_ref, z_ref.at[k], tile_ref.at[k], sems.at[k])
        pending.append(unit(scalars, off_of, plain(own), plain(swapped), own, *refs))
    out_ref[...] = acc_ref[...].astype(out_ref.dtype)
    for one in pending:
        end_tiles(one)


SMEM = pl.BlockSpec(memory_space=pltpu.SMEM)
INSIDE = pl.BlockSpec(memory_space=pltpu.VMEM)
ANY = pl.BlockSpec(memory_space=pl.ANY)


def estimate(mib):
    return pl.CostEstimate(flops=1, bytes_accessed=1 + int(mib * 2**20), transcendentals=0)


EST = {"last": 4, "near": 8, "next": 0, "self": 0.5, "zx_p": 1}


def run_self(ids, table, wins, own, par):
    rows, width = own.shape
    return pl.pallas_call(
        self_kernel,
        out_shape=(
            jax.ShapeDtypeStruct((rows, 2 * width), jnp.bfloat16),
            jax.ShapeDtypeStruct((rows, width), jnp.float32),
            jax.ShapeDtypeStruct((2 * CAP, BS, BS), jnp.float32),
        ),
        in_specs=[SMEM, SMEM, SMEM, INSIDE, INSIDE],
        out_specs=(INSIDE, INSIDE, ANY),
        scratch_shapes=[pltpu.VMEM((CAP, BS, BS), jnp.float32), pltpu.SemaphoreType.DMA((PARTS,))],
        compiler_params=pltpu.CompilerParams(vmem_limit_bytes=VMEM),
        cost_estimate=estimate(EST["self"]),
        name="self_pairs",
    )(ids, table, wins, own, par)


def run_unit(kernel, name, corr, inputs, outs, acc_shape=None, units=None):
    rows, both = inputs[3].shape
    many = (units,) if units else ()
    scratch = [pltpu.VMEM(acc_shape, jnp.float32)] if acc_shape else []
    outs = [jax.ShapeDtypeStruct((rows, width), dtype) for width, dtype in outs]
    return pl.pallas_call(
        kernel,
        out_shape=(*outs, jax.ShapeDtypeStruct(corr.shape, corr.dtype)),
        in_specs=[SMEM] * 3 + [INSIDE] * (len(inputs) - 3) + [ANY],
        out_specs=(*[INSIDE] * len(outs), ANY),
        scratch_shapes=scratch
        + [
            pltpu.VMEM((*many, rows, both), jnp.bfloat16),
            pltpu.VMEM((*many, CAP, BS, BS), jnp.float32),
            pltpu.SemaphoreType.DMA((*many, PARTS)),
        ],
        input_output_aliases={len(inputs): len(outs)},
        compiler_params=pltpu.CompilerParams(vmem_limit_bytes=VMEM),
        cost_estimate=estimate(EST[name[:4]]),
        name=name,
    )(*inputs, corr)


def with_table(spectra, table):
    rows, width = spectra.shape
    below = jnp.pad(table, ((rows, TABLE - 2), (0, width - table.shape[1])))
    below = jnp.where(below >= 0, lax.rem(below, BLK_DEV), -1).astype(spectra.dtype)
    return jnp.pad(spectra, ((0, TABLE), (0, 0))) + below


def body(spectra, pair_blocks, windows):
    hold = lax.optimization_barrier
    position = lax.axis_index("feat")
    rows, width = spectra.shape
    both = 2 * width
    table, wins = pair_blocks.T, windows.T
    unit = with_table(spectra, table)
    par = swap(unit)
    near_own = send(unit, move_near)
    from_z = send(unit, move_z)
    near_par = send(par, move_near)
    ids = jnp.stack([position, lax.axis_index("samp")]).astype(jnp.int32)
    scalars = (ids, table, wins)
    ids, near_own = hold((ids, near_own))
    scalars = (ids, table, wins)
    zown, acc, corr = run_self(ids, table, wins, spectra, par)
    near_own, _ = hold((near_own, acc))
    next_own = send(near_own, move_next)
    near_par, acc = hold((near_par, acc))
    next_par = send(near_par, move_next)
    zx = send(from_z, move_x)
    near_par, acc = hold((near_par, acc))
    acc, corr = run_unit(
        near_kernel,
        "near_pairs",
        corr,
        (*scalars, zown, acc, near_own, near_par),
        [(both, jnp.float32)],
    )
    next_own, _ = hold((next_own, acc))
    last = send(next_own, move_last)
    acc, give, corr = run_unit(
        next_kernel,
        "next_pairs",
        corr,
        (*scalars, zown, acc, next_own, next_par),
        [(width, jnp.float32), (width, jnp.bfloat16)],
        (rows, both),
    )
    zx, acc = hold((zx, acc))
    got = swap(give)
    acc, corr = run_unit(
        both_kernel,
        "zx_pairs",
        corr,
        (*scalars, zown, acc, zx, swap(zx)),
        [(width, jnp.float32)],
    )
    profiles, corr = run_unit(
        last_kernel,
        "last_pairs",
        corr,
        (*scalars, zown, acc, last, swap(last), got),
        [(width, jnp.bfloat16)],
        (rows, width),
    )
    return (corr, profiles)


def solution(mesh):
    placed = (P("feat", "samp"), P("feat", None), P())
    return jax.shard_map(
        body,
        mesh=mesh,
        in_specs=placed,
        out_specs=(P(("feat", "samp"), None, None), P("feat", "samp")),
        check_vma=False,
    )
```

```python
import functools

import jax
import jax.numpy as jnp
from jax import lax
from jax.experimental import pallas as pl
from jax.experimental.pallas import tpu as pltpu
from jax.sharding import PartitionSpec as P

BS = 256
BLK_DEV = 4
CAP = 8
REACH = 3
SLOTS = (REACH + 1) * CAP
QUAD = 4
EPS = 1e-05
STEP = 256
TABLE = 2 * CAP
PARTS = 4
VMEM = 24 * 1024 * 1024


def along_x(i):
    return i ^ 1


def along_y(i):
    return i ^ 2


def along_z_side(i, n):
    return (i + QUAD if i % QUAD < 2 else i - QUAD) % n


def move_near(i, core, n):
    return (along_x(i), 0) if core == 0 else (along_y(i), 1)


def move_z(i, core, n):
    return (i - QUAD if i % 2 == 0 else i + QUAD) % n, core


def move_next(i, core, n):
    if core == 0:
        to = along_y(i)
        return to, (1 if to % QUAD == 0 else 0)
    to = along_z_side(i, n)
    return to, (0 if to % QUAD == 0 else 1)


def move_x(i, core, n):
    return along_x(i), core


def move_last(i, core, n):
    holds_diag = core == (1 if i % QUAD == 0 else 0)
    return (along_z_side(i, n), 0) if holds_diag else (along_x(i), 1)


def send(value, move):
    length, cores = lax.axis_size("feat"), lax.axis_size("samp")
    pairs = []
    for i in range(length):
        for core in range(cores):
            to, to_core = move(i, core, length)
            pairs.append((i * cores + core, to * cores + to_core))
    return lax.ppermute(value, ("feat", "samp"), pairs)


def swap(value):
    return lax.ppermute(value, "samp", [(0, 1), (1, 0)])


def off_near(r, core):
    return jnp.where(core == 0, 1 - 2 * lax.rem(r, 2), 2 - 4 * lax.div(r, 2))


def off_next(r, core):
    return jnp.where((core == 0) != (r == 0), 3 - 2 * r, 4 * lax.div(r, 2) - 2)


def off_zx(r, core):
    return 6 * lax.rem(r, 2) - 3


def off_last(r, core):
    return jnp.where(r == 0, -1, jnp.where(r == 1, -3, jnp.where(r == 2, 3, 1)))


def normalise(read_own, read_par, z_ref):
    rows = z_ref.shape[0]
    width = z_ref.shape[1] // 2
    total = 2 * width
    for at in range(0, rows, STEP):
        here = slice(at, at + STEP)
        a = read_own(here).astype(jnp.float32)
        b = read_par(here).astype(jnp.float32)
        mean = jnp.sum(a + b, axis=1, keepdims=True) / total
        var = jnp.sum(a * a + b * b, axis=1, keepdims=True) / total - mean * mean
        inv = lax.rsqrt(var + EPS)
        z_ref[here, :width] = ((a - mean) * inv).astype(jnp.bfloat16)
        z_ref[here, width:] = ((b - mean) * inv).astype(jnp.bfloat16)


def slot_of(ids, table, wins, off, slot, code):
    position = ids[0]
    ahead = off >= 0
    at = jnp.maximum(off, 0) * CAP + slot
    left = jnp.where(ahead, table[0, at] - position * BLK_DEV, lax.div(code, BLK_DEV))
    right = jnp.where(ahead, table[1, at] - (position + off) * BLK_DEV, lax.rem(code, BLK_DEV))
    live = jnp.where(ahead, table[0, at], code) >= 0
    live = jnp.logical_and(live, position + off >= 0)
    b = jnp.where(live, jnp.where(ahead, left, right), 0)
    o = jnp.where(live, jnp.where(ahead, right, left), 0)
    mine = position * BLK_DEV + b
    other = jnp.where(live, (position + off) * BLK_DEV + o, 0)
    lo_b, hi_b = wins[0, mine], wins[1, mine]
    lo_o, hi_o = wins[0, other], wins[1, other]
    meet = jnp.maximum(jnp.minimum(hi_b, hi_o) - jnp.maximum(lo_b, lo_o), 0)
    num = jnp.where(live, meet + 16, 0)
    den = hi_b - lo_b + hi_o - lo_o + 16
    return b, o, num, den


def codes_of(rows, off):
    values = rows.astype(jnp.float32)
    row = lax.broadcasted_iota(jnp.int32, values.shape, 0)
    values = jnp.where(row == 0, BLK_DEV * values, values)
    lane = lax.broadcasted_iota(jnp.int32, values.shape, 1)
    first = jnp.maximum(-off, 0) * CAP
    return [
        jnp.sum(
            jnp.where(jnp.logical_and(row < 2, lane == first + slot), values, 0.0)
        ).astype(jnp.int32)
        for slot in range(CAP)
    ]


def scale_of(num, den, samples):
    top = jnp.full((1, BS), num, jnp.int32).astype(jnp.float32)
    low = jnp.full((1, BS), den, jnp.int32).astype(jnp.float32)
    return top / low / samples


def at_block(index):
    return pl.ds(pl.multiple_of(index * BS, BS), BS)


def grams(found, zown_ref, z_ref, tile_ref):
    samples = zown_ref.shape[1]
    for slot, (b, o, num, den) in found:
        gram = lax.dot_general(
            zown_ref[at_block(b), :],
            z_ref[at_block(o), :],
            (((1,), (1,)), ((), ())),
            preferred_element_type=jnp.float32,
        )
        tile_ref[slot] = gram * scale_of(num, den, samples)


def products(found, zown_ref, z_ref, tile_ref, acc_ref, itself):
    width = acc_ref.shape[1]
    for slot, (b, o, _, _) in found:
        tile = tile_ref[slot].astype(jnp.bfloat16)
        acc_ref[at_block(b), :] += jnp.dot(
            tile, z_ref[at_block(o), :width], preferred_element_type=jnp.float32
        )
        if itself:
            back = lax.dot_general(
                tile,
                zown_ref[at_block(b), :width],
                (((0,), (0,)), ((), ())),
                preferred_element_type=jnp.float32,
            )
            acc_ref[at_block(o), :] += back * jnp.where(b == o, 0.0, 1.0)


def put_tiles(ids, off, some, tile_ref, corr_ref, sem):
    mine = jnp.logical_and(off >= 0, lax.div(off, 2) == ids[1])
    first = jnp.where(jnp.logical_or(off == 1, off == 3), CAP, 0) + some.start
    copy = pltpu.make_async_copy(
        tile_ref.at[some], corr_ref.at[pl.ds(first, some.stop - some.start)], sem
    )

    @pl.when(mine)
    def _():
        copy.start()

    return mine, copy


def end_tiles(pending):
    for mine, copy in pending:

        @pl.when(mine)
        def _(copy=copy):
            copy.wait()


def grams_out(scalars, off, codes, zown_ref, z_ref, tile_ref, corr_ref, sems):
    found = [(slot, slot_of(*scalars, off, slot, codes[slot])) for slot in range(CAP)]
    pending = []
    for part in range(PARTS):
        some = slice(part * CAP // PARTS, (part + 1) * CAP // PARTS)
        grams(found[some], zown_ref, z_ref, tile_ref)
        pending.append(put_tiles(scalars[0], off, some, tile_ref, corr_ref, sems.at[part]))
    return found, pending


def self_kernel(ids, table, wins, own_ref, par_ref, zown_ref, acc_ref, corr_ref, tile_ref, sems):
    scalars = (ids, table, wins)
    width = own_ref.shape[1]
    normalise(lambda at: own_ref[at, :], lambda at: par_ref[at, :], zown_ref)
    none = [jnp.int32(-1)] * CAP
    found, pending = grams_out(
        scalars, jnp.int32(0), none, zown_ref, zown_ref, tile_ref, corr_ref, sems
    )
    acc_ref[...] = zown_ref[:, :width].astype(jnp.float32)
    products(found, zown_ref, zown_ref, tile_ref, acc_ref, True)
    end_tiles(pending)


def either(first, one_ref, two_ref):
    return lambda at: jnp.where(first, one_ref[at, :], two_ref[at, :])


def plain(ref):
    return lambda at: ref[at, :]


def unit(scalars, off_of, own, par, table_ref, zown_ref, acc_ref, corr_ref, z_ref, tile_ref, sem):
    rows = zown_ref.shape[0]
    ids = scalars[0]
    off = off_of(lax.rem(ids[0], QUAD), ids[1])
    normalise(own, par, z_ref)
    codes = codes_of(table_ref[rows : rows + TABLE, :128], off)
    found, pending = grams_out(scalars, off, codes, zown_ref, z_ref, tile_ref, corr_ref, sem)
    products(found, zown_ref, z_ref, tile_ref, acc_ref, False)
    return pending


def near_kernel(
    ids, table, wins, zown_ref, acc_in, own_ref, par_ref, _, acc_ref, corr_ref, z_ref, tile_ref, sem
):
    scalars = (ids, table, wins)
    width = acc_in.shape[1]
    acc_ref[:, :width] = acc_in[...]
    acc_ref[:, width:] = jnp.zeros_like(acc_in)
    refs = (zown_ref, acc_ref, corr_ref, z_ref, tile_ref, sem)
    end_tiles(unit(scalars, off_near, plain(own_ref), plain(par_ref), own_ref, *refs))


def next_kernel(
    ids, table, wins, zown_ref, acc_in, one_ref, two_ref, _, out_ref, give_ref, corr_ref, *scratch
):
    scalars = (ids, table, wins)
    acc_ref, z_ref, tile_ref, sem = scratch
    width = out_ref.shape[1]
    acc_ref[...] = acc_in[...]
    straight = lax.rem(ids[0], QUAD) != 0
    own, par = either(straight, one_ref, two_ref), either(straight, two_ref, one_ref)
    refs = (zown_ref, acc_ref, corr_ref, z_ref, tile_ref, sem)
    pending = unit(scalars, off_next, own, par, one_ref, *refs)
    out_ref[...] = acc_ref[:, :width]
    give_ref[...] = acc_ref[:, width:].astype(give_ref.dtype)
    end_tiles(pending)


def both_kernel(
    ids, table, wins, zown_ref, acc_in, own_ref, par_ref, _, out_ref, corr_ref, z_ref, tile_ref, sem
):
    scalars = (ids, table, wins)
    out_ref[...] = acc_in[...]
    refs = (zown_ref, out_ref, corr_ref, z_ref, tile_ref, sem)
    end_tiles(unit(scalars, off_zx, plain(own_ref), plain(par_ref), own_ref, *refs))


def last_kernel(
    ids, table, wins, zown_ref, acc_in, own_ref, par_ref, got_ref, _, out_ref, corr_ref, *scratch
):
    scalars = (ids, table, wins)
    acc_ref, z_ref, tile_ref, sem = scratch
    acc_ref[...] = acc_in[...] + got_ref[...].astype(jnp.float32)
    refs = (zown_ref, acc_ref, corr_ref, z_ref, tile_ref, sem)
    pending = unit(scalars, off_last, plain(own_ref), plain(par_ref), own_ref, *refs)
    out_ref[...] = acc_ref[...].astype(out_ref.dtype)
    end_tiles(pending)


def last_two_kernel(
    ids, table, wins, zown_ref, acc_in, zx_ref, zx_par, own_ref, par_ref, got_ref, _, out_ref, corr_ref, *scratch
):
    scalars = (ids, table, wins)
    acc_ref, z_ref, tile_ref, sems = scratch
    acc_ref[...] = acc_in[...] + got_ref[...].astype(jnp.float32)
    pending = []
    for k, (off_of, own, swapped) in enumerate(
        ((off_zx, zx_ref, zx_par), (off_last, own_ref, par_ref))
    ):
        refs = (zown_ref, acc_ref, corr_ref, z_ref.at[k], tile_ref.at[k], sems.at[k])
        pending.append(unit(scalars, off_of, plain(own), plain(swapped), own, *refs))
    out_ref[...] = acc_ref[...].astype(out_ref.dtype)
    for one in pending:
        end_tiles(one)


SMEM = pl.BlockSpec(memory_space=pltpu.SMEM)
INSIDE = pl.BlockSpec(memory_space=pltpu.VMEM)
ANY = pl.BlockSpec(memory_space=pl.ANY)


def estimate(mib):
    return pl.CostEstimate(flops=1, bytes_accessed=1 + int(mib * 2**20), transcendentals=0)


EST = {"last": 4, "near": 8, "next": 0, "self": 0.5, "zx_p": 1}


def run_self(ids, table, wins, own, par):
    rows, width = own.shape
    return pl.pallas_call(
        self_kernel,
        out_shape=(
            jax.ShapeDtypeStruct((rows, 2 * width), jnp.bfloat16),
            jax.ShapeDtypeStruct((rows, width), jnp.float32),
            jax.ShapeDtypeStruct((2 * CAP, BS, BS), jnp.float32),
        ),
        in_specs=[SMEM, SMEM, SMEM, INSIDE, INSIDE],
        out_specs=(INSIDE, INSIDE, ANY),
        scratch_shapes=[pltpu.VMEM((CAP, BS, BS), jnp.float32), pltpu.SemaphoreType.DMA((PARTS,))],
        compiler_params=pltpu.CompilerParams(vmem_limit_bytes=VMEM),
        cost_estimate=estimate(EST["self"]),
        name="self_pairs",
    )(ids, table, wins, own, par)


def run_unit(kernel, name, corr, inputs, outs, acc_shape=None, units=None):
    rows, both = inputs[3].shape
    many = (units,) if units else ()
    scratch = [pltpu.VMEM(acc_shape, jnp.float32)] if acc_shape else []
    outs = [jax.ShapeDtypeStruct((rows, width), dtype) for width, dtype in outs]
    return pl.pallas_call(
        kernel,
        out_shape=(*outs, jax.ShapeDtypeStruct(corr.shape, corr.dtype)),
        in_specs=[SMEM] * 3 + [INSIDE] * (len(inputs) - 3) + [ANY],
        out_specs=(*[INSIDE] * len(outs), ANY),
        scratch_shapes=scratch
        + [
            pltpu.VMEM((*many, rows, both), jnp.bfloat16),
            pltpu.VMEM((*many, CAP, BS, BS), jnp.float32),
            pltpu.SemaphoreType.DMA((*many, PARTS)),
        ],
        input_output_aliases={len(inputs): len(outs)},
        compiler_params=pltpu.CompilerParams(vmem_limit_bytes=VMEM),
        cost_estimate=estimate(EST[name[:4]]),
        name=name,
    )(*inputs, corr)


def with_table(spectra, table):
    rows, width = spectra.shape
    below = jnp.pad(table, ((rows, TABLE - 2), (0, width - table.shape[1])))
    below = jnp.where(below >= 0, lax.rem(below, BLK_DEV), -1).astype(spectra.dtype)
    return jnp.pad(spectra, ((0, TABLE), (0, 0))) + below


def body(spectra, pair_blocks, windows):
    hold = lax.optimization_barrier
    position = lax.axis_index("feat")
    rows, width = spectra.shape
    both = 2 * width
    table, wins = pair_blocks.T, windows.T
    unit = with_table(spectra, table)
    par = swap(unit)
    near_own = send(unit, move_near)
    from_z = send(unit, move_z)
    near_par = send(par, move_near)
    ids = jnp.stack([position, lax.axis_index("samp")]).astype(jnp.int32)
    scalars = (ids, table, wins)
    ids, near_own = hold((ids, near_own))
    scalars = (ids, table, wins)
    zown, acc, corr = run_self(ids, table, wins, spectra, par)
    near_own, _ = hold((near_own, acc))
    next_own = send(near_own, move_next)
    near_par, acc = hold((near_par, acc))
    next_par = send(near_par, move_next)
    zx = send(from_z, move_x)
    near_par, acc = hold((near_par, acc))
    acc, corr = run_unit(
        near_kernel,
        "near_pairs",
        corr,
        (*scalars, zown, acc, near_own, near_par),
        [(both, jnp.float32)],
    )
    next_own, _ = hold((next_own, acc))
    last = send(next_own, move_last)
    acc, give, corr = run_unit(
        next_kernel,
        "next_pairs",
        corr,
        (*scalars, zown, acc, next_own, next_par),
        [(width, jnp.float32), (width, jnp.bfloat16)],
        (rows, both),
    )
    zx, acc = hold((zx, acc))
    got = swap(give)
    acc, corr = run_unit(
        both_kernel,
        "zx_pairs",
        corr,
        (*scalars, zown, acc, zx, swap(zx)),
        [(width, jnp.float32)],
    )
    profiles, corr = run_unit(
        last_kernel,
        "last_pairs",
        corr,
        (*scalars, zown, acc, last, swap(last), got),
        [(width, jnp.bfloat16)],
        (rows, width),
    )
    return (corr, profiles)


def solution(mesh):
    placed = (P("feat", "samp"), P("feat", None), P())
    return jax.shard_map(
        body,
        mesh=mesh,
        in_specs=placed,
        out_specs=(P(("feat", "samp"), None, None), P("feat", "samp")),
        check_vma=False,
    )
```
